128 devices in a mesh: panel: 16 (over x, z_lo, core), rep: 8 (over y, z_hi).
Axes of the slice: x: 4, y: 4, z: 4 (z_hi: 2, z_lo: 2; z = z_hi * 2 + z_lo), core: 2. Of those that a mesh axis runs over, the one named last changes fastest.
Arguments:
- activations: float32 [393216, 1024], P(('panel', 'rep')), may hold values from 0 to 48
- out_grads: float32 [393216, 256], P(('panel', 'rep')), may hold values from -8 to 8
- factor_a: float32 [1024, 1024], P('panel'), may hold values from -7 to 27
- factor_g: float32 [256, 256], P('panel'), may hold values from -7 to 27
- inverse_a: float32 [1024, 1024], P('panel'), may hold values from -0.1875 to 0.1875
- inverse_g: float32 [256, 256], P('panel'), may hold values from -0.375 to 0.375
Outputs:
- new_factor_a: float32 [1024, 1024], P('panel')
- new_factor_g: float32 [256, 256], P('panel')
- precond_grad: float32 [1024, 256], P('panel')
The draws below stay inside these ranges and needn't reach their ends.
All inputs are finite; a program needn't handle non-finite values.
Results may differ from the reference program's by a relative error of at most 0.000076.
Values sent between devices are 32-bit elements; how exact they have to be, the bound alone decides.
No kernel may reach another device: no remote copies, remote signals or barrier semaphores. Data moves between devices by JAX's collectives and lax.ppermute only.
A program may use at most 128 MiB of HBM per device.

```python
import math
import jax
import jax.numpy as jnp
from jax import lax

CIN = 1024
COUT = 256
ROWS_DEV = 3072
ROWS = 393216


def channel_scales(key):
    lower_log = math.log(0.3)
    upper_log = math.log(3.0)
    input_scale = jnp.exp(jax.random.uniform(jax.random.fold_in(key, 11), (CIN,), jnp.float32, lower_log, upper_log))
    output_scale = jnp.exp(jax.random.uniform(jax.random.fold_in(key, 12), (COUT,), jnp.float32, lower_log, upper_log))
    return (input_scale, output_scale)


def row_scales(key):
    return jnp.exp(jax.random.uniform(key, (ROWS, 1), jnp.float32, math.log(0.3), math.log(3.0)))


def draw_activations(key, part):
    input_scale, output_scale = channel_scales(key)
    base_key = jax.random.fold_in(key, 21)
    block_count = ROWS // ROWS_DEV
    row_scale = row_scales(jax.random.fold_in(base_key, 1))
    loading = jax.random.uniform(jax.random.fold_in(base_key, 2), (1, CIN), jnp.float32, 0.0, 1.0)
    shared_factor = jnp.clip(jax.random.normal(jax.random.fold_in(base_key, 3), (ROWS, 1), jnp.float32), -3.0, 3.0)
    block_means = jax.random.uniform(jax.random.fold_in(base_key, 4), (block_count, 1, CIN), jnp.float32, 0.2, 1.5)
    noise_part = jnp.clip(jax.random.normal(jax.random.fold_in(base_key, 5), (block_count, ROWS_DEV, CIN), jnp.float32), -3.0, 3.0)
    shrink_by = 1.0 / 1.5
    inner_sum = (block_means + noise_part).reshape(ROWS, CIN) + shared_factor * loading
    values = row_scale * input_scale[None, :] * jnp.maximum(inner_sum, 0.0) * shrink_by
    return values.astype(jnp.float32)


def draw_out_grads(key, part):
    input_scale, output_scale = channel_scales(key)
    base_key = jax.random.fold_in(key, 31)
    block_count = ROWS // ROWS_DEV
    row_scale = row_scales(jax.random.fold_in(base_key, 1))
    shared_factor = jnp.clip(jax.random.normal(jax.random.fold_in(base_key, 2), (ROWS, 1), jnp.float32), -3.0, 3.0)
    loading = jnp.clip(jax.random.normal(jax.random.fold_in(base_key, 3), (1, COUT), jnp.float32), -3.0, 3.0)
    block_dirs = jnp.clip(jax.random.normal(jax.random.fold_in(base_key, 4), (block_count, 1, COUT), jnp.float32), -3.0, 3.0)
    noise_part = jnp.clip(jax.random.normal(jax.random.fold_in(base_key, 5), (block_count, ROWS_DEV, COUT), jnp.float32), -3.0, 3.0)
    inner_sum = (0.7 * block_dirs + noise_part).reshape(ROWS, COUT) + shared_factor * loading
    values = row_scale * output_scale[None, :] * inner_sum / math.sqrt(ROWS)
    return values.astype(jnp.float32)


def symmetric_factor(key, scale_vector, order):
    entries = jnp.clip(jax.random.normal(key, (order, order), jnp.float32), -3.0, 3.0)
    mixed = (entries + entries.T) * 0.7071
    outer_scale = scale_vector[:, None] * scale_vector[None, :]
    values = outer_scale * (0.6 + 0.3 * mixed) + jnp.eye(order, dtype=jnp.float32) * outer_scale
    return values.astype(jnp.float32)


def draw_factor_a(key, part):
    input_scale, output_scale = channel_scales(key)
    return symmetric_factor(jax.random.fold_in(key, 41), input_scale, CIN)


def draw_factor_g(key, part):
    input_scale, output_scale = channel_scales(key)
    return symmetric_factor(jax.random.fold_in(key, 51), output_scale, COUT)


def shard_levels(stream_key, extent, pieces, smallest, largest):
    factor_of = 1.0
    for position, blocks in pieces:
        steps = jax.random.uniform(jax.random.fold_in(jax.random.fold_in(stream_key, 6), position), (blocks,), jnp.float32, smallest / len(pieces), largest / len(pieces))
        factor_of = factor_of * jnp.repeat(jnp.exp(steps), extent[position] // blocks).reshape((-1,) + (1,) * (len(extent) - 1 - position))
    return factor_of


def scatter_about(key, dims, width, limit, shards=(), kind=jnp.bfloat16):
    gain = shard_levels(key, dims, shards, -0.22, 0.18) if shards else 1.0
    values = jax.random.normal(key, dims, jnp.float32) * width * gain
    return jnp.minimum(jnp.maximum(values, -limit), limit).astype(kind)


def setup_inputs(seed: int = 0) -> dict:
    key_list = jax.random.split(jax.random.key(seed), 7)
    activations = draw_activations(jax.random.fold_in(key_list[6], 71), 0)
    out_grads = draw_out_grads(jax.random.fold_in(key_list[6], 71), 0)
    factor_a = draw_factor_a(jax.random.fold_in(key_list[6], 71), 0)
    factor_g = draw_factor_g(jax.random.fold_in(key_list[6], 71), 0)
    inverse_a = scatter_about(key_list[4], (CIN, CIN), CIN ** -0.5, 0.1875, ((0, 16),), jnp.float32)
    inverse_g = scatter_about(key_list[5], (COUT, COUT), COUT ** -0.5, 0.375, ((0, 16),), jnp.float32)
    return dict(activations=activations, out_grads=out_grads, factor_a=factor_a, factor_g=factor_g, inverse_a=inverse_a, inverse_g=inverse_g)


decay_rate = 0.6


def reference(activations, out_grads, factor_a, factor_g, inverse_a, inverse_g):
    highest = lax.Precision.HIGHEST
    contract = (((0,), (0,)), ((), ()))
    stat_a = lax.dot_general(activations, activations, contract, precision=highest, preferred_element_type=jnp.float32) / ROWS
    stat_g = lax.dot_general(out_grads, out_grads, contract, precision=highest, preferred_element_type=jnp.float32)
    grad = lax.dot_general(activations, out_grads, contract, precision=highest, preferred_element_type=jnp.float32)
    new_factor_a = decay_rate * factor_a + (1.0 - decay_rate) * stat_a
    new_factor_g = decay_rate * factor_g + (1.0 - decay_rate) * stat_g
    right = jnp.dot(grad, inverse_g, precision=highest, preferred_element_type=jnp.float32)
    precond_grad = jnp.dot(inverse_a, right, precision=highest, preferred_element_type=jnp.float32)
    return new_factor_a, new_factor_g, precond_grad
```

```python
import functools

import jax
import jax.numpy as jnp
from jax import lax
from jax.experimental import pallas as pl
from jax.experimental.pallas import tpu as pltpu
from jax.sharding import PartitionSpec as P

decay_rate = 0.6
F32 = jnp.float32
BF16 = jnp.bfloat16
SUB = ("x", "zl", "co", "y", "zh")
SIZES = (4, 2, 2, 4, 2)
CHIPS = ("x", "zl", "y", "zh")
VMEM = 58 * 2**20


def split(block):
    high = block.astype(BF16)
    return high, (block - high.astype(F32)).astype(BF16)


def gram(left, right):
    return lax.dot_general(left, right, (((0,), (0,)), ((), ())), preferred_element_type=F32)


def gram3(lh, ll, rh, rl):
    return gram(lh, rh) + gram(lh, rl) + gram(ll, rh)


def grad_kernel(core_ref, a_ref, g_ref, mine_ref, other_ref, grad, small):
    step = pl.program_id(0)
    gh, gl = split(g_ref[...])
    ah, al = split(a_ref[...])

    @pl.when(step == 0)
    def _():
        grad[...] = jnp.zeros_like(grad)
        small[...] = jnp.zeros_like(small)

    for j in range(0, grad.shape[0], 256):
        c = slice(j, j + 256)
        grad[c, :] += gram3(ah[:, c], al[:, c], gh, gl)
    small[...] += gram3(gh, gl, gh, gl)

    @pl.when(step == pl.num_programs(0) - 1)
    def _():
        core = core_ref[0]
        for which, out in ((core, mine_ref), (1 - core, other_ref)):
            for q in range(8):
                owner = 2 * q + which
                rows = pl.ds(pl.multiple_of(owner * 64, 64), 64)
                for half in range(2):
                    cols = slice(half * 128, half * 128 + 128)
                    tile = slice(half * 8, half * 8 + 8)
                    out[q * 8 : q * 8 + 8, tile, :] = grad[rows, cols].reshape(8, 8, 128)
                for y in range(4):
                    srows = pl.ds(pl.multiple_of(owner * 16 + 8 * (y // 2), 8), 8)
                    part = small[srows, 128 * (y % 2) : 128 * (y % 2) + 128]
                    out[q * 8 + 2 * y, 16:24, :] = part
                    out[q * 8 + 2 * y + 1, 16:24, :] = part


def grad_parts(core, activations, out_grads):
    rows, cin = activations.shape
    cout = out_grads.shape[1]
    tile = 512
    shape = jax.ShapeDtypeStruct((64, 24, 128), F32)
    spec = pl.BlockSpec((64, 24, 128), lambda k: (0, 0, 0))
    return pl.pallas_call(
        grad_kernel,
        grid=(rows // tile,),
        in_specs=[
            pl.BlockSpec(memory_space=pltpu.SMEM),
            pl.BlockSpec((tile, cin), lambda k: (k, 0)),
            pl.BlockSpec((tile, cout), lambda k: (k, 0)),
        ],
        out_specs=[spec, spec],
        out_shape=[shape, shape],
        scratch_shapes=[pltpu.VMEM((cin, cout), F32), pltpu.VMEM((cout, cout), F32)],
        compiler_params=pltpu.CompilerParams(vmem_limit_bytes=VMEM),
        cost_estimate=pl.CostEstimate(flops=6 * rows * (cin + cout) * cout, bytes_accessed=4 * rows * (cin + cout), transcendentals=0),
        name="grad_parts",
    )(core, activations, out_grads)


def stat_kernel(core_ref, a_ref, mine_ref, other_ref, acc):
    step = pl.program_id(0)
    cin = acc.shape[0]
    ah, al = split(a_ref[...])

    @pl.when(step == 0)
    def _():
        acc[...] = jnp.zeros_like(acc)

    for i in range(0, cin, 256):
        ci, cj = slice(i, i + 256), slice(i, cin)
        acc[ci, cj] += gram3(ah[:, ci], al[:, ci], ah[:, cj], al[:, cj])

    @pl.when(step == pl.num_programs(0) - 1)
    def _():
        for i in range(0, cin, 256):
            for j in range(i + 256, cin, 256):
                acc[j : j + 256, i : i + 256] = acc[i : i + 256, j : j + 256].T
        core = core_ref[0]
        for which, out in ((core, mine_ref), (1 - core, other_ref)):
            for q in range(8):
                rows = pl.ds(pl.multiple_of((2 * q + which) * 64, 64), 64)
                out[q * 64 : q * 64 + 64, :] = acc[rows, :]


def stat_parts(core, activations):
    rows, cin = activations.shape
    tile = 512
    shape = jax.ShapeDtypeStruct((cin // 2, cin), F32)
    spec = pl.BlockSpec((cin // 2, cin), lambda k: (0, 0))
    return pl.pallas_call(
        stat_kernel,
        grid=(rows // tile,),
        in_specs=[
            pl.BlockSpec(memory_space=pltpu.SMEM),
            pl.BlockSpec((tile, cin), lambda k: (k, 0)),
        ],
        out_specs=[spec, spec],
        out_shape=[shape, shape],
        scratch_shapes=[pltpu.VMEM((cin, cin), F32)],
        compiler_params=pltpu.CompilerParams(vmem_limit_bytes=VMEM),
        cost_estimate=pl.CostEstimate(flops=4 * rows * cin * cin, bytes_accessed=4 * rows * cin, transcendentals=0),
        name="stat_parts",
    )(core, activations)


def final_kernel(inv_a_ref, grad_ref, inv_g_ref, out_ref):
    halves = [grad_ref[:, 8 * h : 8 * h + 8, :].reshape(1024, 128) for h in range(2)]
    grad = jnp.concatenate(halves, axis=1)
    left = jnp.dot(inv_a_ref[...], grad, precision=lax.Precision.HIGHEST, preferred_element_type=F32)
    out_ref[...] = jnp.dot(left, inv_g_ref[...], precision=lax.Precision.HIGHEST, preferred_element_type=F32)


def final(inverse_a, grad, inverse_g):
    return pl.pallas_call(
        final_kernel,
        out_shape=jax.ShapeDtypeStruct((inverse_a.shape[0], 256), F32),
        compiler_params=pltpu.CompilerParams(vmem_limit_bytes=VMEM),
        name="final",
    )(inverse_a, grad, inverse_g)


def pairs(move):
    index = lambda c: (((c[0] * 2 + c[1]) * 2 + c[2]) * 4 + c[3]) * 2 + c[4]
    out = []
    for flat in range(128):
        zh, rest = flat % 2, flat // 2
        y, rest = rest % 4, rest // 4
        co, rest = rest % 2, rest // 2
        zl, x = rest % 2, rest // 2
        out.append((flat, index(move(x, zl, co, y, zh))))
    return out


CORE = pairs(lambda x, zl, co, y, zh: (x, zl, 1 - co, y, zh))
Z1 = pairs(lambda x, zl, co, y, zh: (x, 1 - zl, co, y, zh))
Z2 = pairs(lambda x, zl, co, y, zh: (x, 1 - zl, co, y, 1 - zh))
Y1 = pairs(lambda x, zl, co, y, zh: (x, zl, co, y ^ 1, zh))
Y2 = pairs(lambda x, zl, co, y, zh: (x, zl, co, 3 - y, zh))
X1 = pairs(lambda x, zl, co, y, zh: (x ^ 1, zl, co, y, zh))
X2 = pairs(lambda x, zl, co, y, zh: (3 - x, zl, co, y, zh))


def move(array, table):
    return lax.ppermute(array, SUB, table)


def join(array, table, axis, late):
    got = move(array, table)
    return jnp.concatenate([jnp.where(late, got, array), jnp.where(late, array, got)], axis=axis)


def local(activations, out_grads, factor_a, factor_g, inverse_a, inverse_g):
    total_rows = activations.shape[0] * 128
    x, zl, co, y, zh = (lax.axis_index(n) for n in SUB)
    core = co.astype(jnp.int32).reshape(1)

    padded = jnp.pad(inverse_g, ((0, 48), (0, 0)))
    inv_g = lax.all_gather(padded, ("x", "zl", "co"), axis=0, tiled=False)[:, :16].reshape(256, 256)

    g_mine, g_other = grad_parts(core, activations, out_grads)
    g_sum = g_mine + move(g_other, CORE)
    g_all = lax.all_to_all(g_sum, CHIPS, 0, 0, tiled=True)
    s_mine, s_other = stat_parts(core, activations)
    s_sum = s_mine + move(s_other, CORE)
    g_own = jnp.sum(g_all, axis=0)
    s_all = lax.all_to_all(s_sum.reshape(64, 8, 1024), CHIPS, 0, 0, tiled=True)

    block = g_own[:16].reshape(1, 1, 1, 1, 1, 16, 128)
    block = join(block, Z1, 1, zl == 1)
    block = join(block, Z2, 4, zh == 1)
    block = join(block, Y1, 3, y % 2 == 1)
    block = join(block, Y2, 3, y >= 2)
    block = join(block, X1, 0, x % 2 == 1)
    block = join(block, X2, 0, x >= 2)
    block = join(block, CORE, 2, co == 1)
    precond_grad = final(inverse_a, block.reshape(128, 16, 128), inv_g)

    s_own = jnp.concatenate([jnp.sum(s_all, axis=0), g_own[16:]], axis=1)
    spread = jnp.broadcast_to(s_own[None], (8,) + s_own.shape)
    rows = lax.all_to_all(spread, ("y", "zh"), 0, 0, tiled=True)
    stat_a = rows[:, :, :1024].reshape(64, 1024) / total_rows
    tiles = rows[::2, :, 1024:].reshape(2, 2, 8, 128)
    stat_g = tiles.transpose(0, 2, 1, 3).reshape(16, 256)
    new_factor_a = decay_rate * factor_a + (1.0 - decay_rate) * stat_a
    new_factor_g = decay_rate * factor_g + (1.0 - decay_rate) * stat_g
    return new_factor_a, new_factor_g, precond_grad


def solution(mesh):
    fine = jax.sharding.Mesh(mesh.devices.reshape(SIZES), SUB)
    rows = P(SUB, None)
    panel = P(("x", "zl", "co"), None)
    return jax.shard_map(
        local,
        mesh=fine,
        in_specs=(rows, rows, panel, panel, panel, panel),
        out_specs=(panel, panel, panel),
        check_vma=False,
    )
```

```python
import functools

import jax
import jax.numpy as jnp
from jax import lax
from jax.experimental import pallas as pl
from jax.experimental.pallas import tpu as pltpu
from jax.sharding import PartitionSpec as P

decay_rate = 0.6
F32 = jnp.float32
BF16 = jnp.bfloat16
SUB = ("x", "zl", "co", "y", "zh")
SIZES = (4, 2, 2, 4, 2)
CHIPS = ("x", "zl", "y", "zh")
CHUNKS = 6
DEPTH = 2


def split(block):
    high = block.astype(BF16)
    return high, (block - high.astype(F32)).astype(BF16)


def gram(left, right):
    return lax.dot_general(left, right, (((0,), (0,)), ((), ())), preferred_element_type=F32)


def gram3(lh, ll, rh, rl):
    return gram(lh, rh) + gram(lh, rl) + gram(ll, rh)


def grad_kernel(core_ref, a_hbm, g_hbm, mine_ref, other_ref, abuf, gbuf, grad, small, sems):
    rows, cin = abuf.shape
    tile = rows // CHUNKS
    copies = []
    for k in range(CHUNKS):
        r = slice(k * tile, k * tile + tile)
        copies.append(
            (
                pltpu.make_async_copy(g_hbm.at[r], gbuf.at[r], sems.at[2 * k]),
                pltpu.make_async_copy(a_hbm.at[r], abuf.at[r], sems.at[2 * k + 1]),
            )
        )
    for k in range(DEPTH):
        for copy in copies[k]:
            copy.start()
    for k in range(CHUNKS):
        r = slice(k * tile, k * tile + tile)
        for copy in copies[k]:
            copy.wait()
        if k + DEPTH < CHUNKS:
            for copy in copies[k + DEPTH]:
                copy.start()
        gh, gl = split(gbuf[r, :])
        ah, al = split(abuf[r, :])
        for j in range(0, cin, 256):
            c = slice(j, j + 256)
            part = gram3(ah[:, c], al[:, c], gh, gl)
            grad[c, :] = part if k == 0 else grad[c, :] + part
        part = gram3(gh, gl, gh, gl)
        small[...] = part if k == 0 else small[...] + part

    core = core_ref[0]
    for which, out in ((core, mine_ref), (1 - core, other_ref)):
        for q in range(8):
            owner = 2 * q + which
            own = pl.ds(pl.multiple_of(owner * 64, 64), 64)
            for half in range(2):
                cols = slice(half * 128, half * 128 + 128)
                place = slice(half * 8, half * 8 + 8)
                out[q * 8 : q * 8 + 8, place, :] = grad[own, cols].reshape(8, 8, 128)
            for y in range(4):
                srows = pl.ds(pl.multiple_of(owner * 16 + 8 * (y // 2), 8), 8)
                part = small[srows, 128 * (y % 2) : 128 * (y % 2) + 128]
                out[q * 8 + 2 * y, 16:24, :] = part
                out[q * 8 + 2 * y + 1, 16:24, :] = part


def grad_parts(core, activations, out_grads):
    rows, cin = activations.shape
    cout = out_grads.shape[1]
    shape = jax.ShapeDtypeStruct((64, 24, 128), F32)
    hbm = pl.BlockSpec(memory_space=pltpu.HBM)
    vmem = pl.BlockSpec(memory_space=pltpu.VMEM)
    return pl.pallas_call(
        grad_kernel,
        in_specs=[pl.BlockSpec(memory_space=pltpu.SMEM), hbm, hbm],
        out_specs=[vmem] * 2,
        out_shape=[shape, shape],
        scratch_shapes=[
            pltpu.VMEM((rows, cin), F32),
            pltpu.VMEM((rows, cout), F32),
            pltpu.VMEM((cin, cout), F32),
            pltpu.VMEM((cout, cout), F32),
            pltpu.SemaphoreType.DMA((2 * CHUNKS,)),
        ],
        compiler_params=pltpu.CompilerParams(vmem_limit_bytes=56 * 2**20),
        cost_estimate=pl.CostEstimate(flops=6 * rows * (cin + cout) * cout, bytes_accessed=4 * rows * (cin + cout), transcendentals=0),
        name="grad_parts",
    )(core, activations, out_grads)


def stat_kernel(core_ref, a_hbm, mine_ref, other_ref, buf, ah, al, acc, sems):
    cin = acc.shape[0]
    count = cin // 256
    copies = [
        pltpu.make_async_copy(a_hbm.at[:, j * 256 : j * 256 + 256], buf.at[j], sems.at[j]) for j in range(count)
    ]
    for copy in copies[:DEPTH]:
        copy.start()
    for j in range(count):
        copies[j].wait()
        if j + DEPTH < count:
            copies[j + DEPTH].start()
        cj = slice(j * 256, j * 256 + 256)
        ah[:, cj], al[:, cj] = split(buf[j])
        for i in range(j + 1):
            ci = slice(i * 256, i * 256 + 256)
            acc[ci, cj] = gram3(ah[:, ci], al[:, ci], ah[:, cj], al[:, cj])
            if i < j:
                acc[cj, ci] = acc[ci, cj].T
    core = core_ref[0]
    for which, out in ((core, mine_ref), (1 - core, other_ref)):
        for q in range(8):
            own = pl.ds(pl.multiple_of((2 * q + which) * 64, 64), 64)
            out[q * 64 : q * 64 + 64, :] = acc[own, :]


def stat_parts(core, activations):
    rows, cin = activations.shape
    shape = jax.ShapeDtypeStruct((cin // 2, cin), F32)
    vmem = pl.BlockSpec(memory_space=pltpu.VMEM)
    return pl.pallas_call(
        stat_kernel,
        in_specs=[pl.BlockSpec(memory_space=pltpu.SMEM), pl.BlockSpec(memory_space=pltpu.HBM)],
        out_specs=[vmem, vmem],
        out_shape=[shape, shape],
        scratch_shapes=[
            pltpu.VMEM((cin // 256, rows, 256), F32),
            pltpu.VMEM((rows, cin), BF16),
            pltpu.VMEM((rows, cin), BF16),
            pltpu.VMEM((cin, cin), F32),
            pltpu.SemaphoreType.DMA((cin // 256,)),
        ],
        compiler_params=pltpu.CompilerParams(vmem_limit_bytes=52 * 2**20),
        cost_estimate=pl.CostEstimate(flops=4 * rows * cin * cin, bytes_accessed=4 * rows * cin, transcendentals=0),
        name="stat_parts",
    )(core, activations)


def final_kernel(inv_a_ref, grad_ref, inv_g_ref, out_ref):
    halves = [grad_ref[:, 8 * h : 8 * h + 8, :].reshape(1024, 128) for h in range(2)]
    grad = jnp.concatenate(halves, axis=1)
    left = jnp.dot(inv_a_ref[...], grad, precision=lax.Precision.HIGHEST, preferred_element_type=F32)
    out_ref[...] = jnp.dot(left, inv_g_ref[...], precision=lax.Precision.HIGHEST, preferred_element_type=F32)


def final(inverse_a, grad, inverse_g):
    return pl.pallas_call(
        final_kernel,
        out_shape=jax.ShapeDtypeStruct((inverse_a.shape[0], 256), F32),
        compiler_params=pltpu.CompilerParams(vmem_limit_bytes=16 * 2**20),
        name="final",
    )(inverse_a, grad, inverse_g)


def pairs(move):
    index = lambda c: (((c[0] * 2 + c[1]) * 2 + c[2]) * 4 + c[3]) * 2 + c[4]
    out = []
    for flat in range(128):
        zh, rest = flat % 2, flat // 2
        y, rest = rest % 4, rest // 4
        co, rest = rest % 2, rest // 2
        zl, x = rest % 2, rest // 2
        out.append((flat, index(move(x, zl, co, y, zh))))
    return out


CORE = pairs(lambda x, zl, co, y, zh: (x, zl, 1 - co, y, zh))
Z1 = pairs(lambda x, zl, co, y, zh: (x, 1 - zl, co, y, zh))
Z2 = pairs(lambda x, zl, co, y, zh: (x, 1 - zl, co, y, 1 - zh))
Y1 = pairs(lambda x, zl, co, y, zh: (x, zl, co, y ^ 1, zh))
Y2 = pairs(lambda x, zl, co, y, zh: (x, zl, co, 3 - y, zh))
X1 = pairs(lambda x, zl, co, y, zh: (x ^ 1, zl, co, y, zh))
X2 = pairs(lambda x, zl, co, y, zh: (3 - x, zl, co, y, zh))


def move(array, table):
    return lax.ppermute(array, SUB, table)


def join(array, table, axis, late):
    got = move(array, table)
    return jnp.concatenate([jnp.where(late, got, array), jnp.where(late, array, got)], axis=axis)


def local(activations, out_grads, factor_a, factor_g, inverse_a, inverse_g):
    total_rows = activations.shape[0] * 128
    x, zl, co, y, zh = (lax.axis_index(n) for n in SUB)
    core = co.astype(jnp.int32).reshape(1)

    padded = jnp.pad(inverse_g, ((0, 48), (0, 0)))
    inv_g = lax.all_gather(padded, ("x", "zl", "co"), axis=0, tiled=False)[:, :16].reshape(256, 256)

    g_mine, g_other = grad_parts(core, activations, out_grads)
    g_sum = g_mine + move(g_other, CORE)
    g_sum, core = lax.optimization_barrier((g_sum, core))
    g_all = lax.all_to_all(g_sum, CHIPS, 0, 0, tiled=True)
    s_mine, s_other = stat_parts(core, activations)
    g_all, s_mine, s_other = lax.optimization_barrier((g_all, s_mine, s_other))
    s_sum = s_mine + move(s_other, CORE)
    g_own = jnp.sum(g_all, axis=0)
    s_all = lax.all_to_all(s_sum.reshape(64, 8, 1024), CHIPS, 0, 0, tiled=True)

    block = g_own[:16].reshape(1, 1, 1, 1, 1, 16, 128)
    block = join(block, Z1, 1, zl == 1)
    block = join(block, Z2, 4, zh == 1)
    block = join(block, Y1, 3, y % 2 == 1)
    block = join(block, Y2, 3, y >= 2)
    block = join(block, X1, 0, x % 2 == 1)
    block = join(block, X2, 0, x >= 2)
    block = join(block, CORE, 2, co == 1)
    precond_grad = final(inverse_a, block.reshape(128, 16, 128), inv_g)

    s_own = jnp.concatenate([jnp.sum(s_all, axis=0), g_own[16:]], axis=1)
    spread = jnp.broadcast_to(s_own[None], (8,) + s_own.shape)
    rows = lax.all_to_all(spread, ("y", "zh"), 0, 0, tiled=True)
    stat_a = rows[:, :, :1024].reshape(64, 1024) / total_rows
    tiles = rows[::2, :, 1024:].reshape(2, 2, 8, 128)
    stat_g = tiles.transpose(0, 2, 1, 3).reshape(16, 256)
    new_factor_a = decay_rate * factor_a + (1.0 - decay_rate) * stat_a
    new_factor_g = decay_rate * factor_g + (1.0 - decay_rate) * stat_g
    return new_factor_a, new_factor_g, precond_grad


def solution(mesh):
    fine = jax.sharding.Mesh(mesh.devices.reshape(SIZES), SUB)
    rows = P(SUB, None)
    panel = P(("x", "zl", "co"), None)
    return jax.shard_map(
        local,
        mesh=fine,
        in_specs=(rows, rows, panel, panel, panel, panel),
        out_specs=(panel, panel, panel),
        check_vma=False,
    )
```

```python
import jax
import jax.numpy as jnp
from jax import lax
from jax.experimental import pallas as pl
from jax.experimental.pallas import tpu as pltpu
from jax.sharding import PartitionSpec as P

decay_rate = 0.6
F32 = jnp.float32
BF16 = jnp.bfloat16
SUB = ("x", "zl", "co", "y", "zh")
SIZES = (4, 2, 2, 4, 2)
CHIPS = ("x", "zl", "y", "zh")
CHUNKS = 6
DEPTH = 2


def split(block):
    high = block.astype(BF16)
    return high, (block - high.astype(F32)).astype(BF16)


def gram(left, right):
    return lax.dot_general(left, right, (((0,), (0,)), ((), ())), preferred_element_type=F32)


def gram3(lh, ll, rh, rl):
    return gram(lh, rh) + gram(lh, rl) + gram(ll, rh)


def in_hbm():
    return pl.BlockSpec(memory_space=pltpu.HBM)


def in_vmem():
    return pl.BlockSpec(memory_space=pltpu.VMEM)


def in_smem():
    return pl.BlockSpec(memory_space=pltpu.SMEM)


def grad_kernel(core_ref, a_hbm, g_hbm, mine_ref, other_ref, abuf, gbuf, ah, al, gh, gl, grad, small, sems):
    rows, cin = abuf.shape
    tile = rows // CHUNKS
    copies = []
    for k in range(CHUNKS):
        r = slice(k * tile, k * tile + tile)
        copies.append(
            (
                pltpu.make_async_copy(g_hbm.at[r], gbuf.at[r], sems.at[2 * k]),
                pltpu.make_async_copy(a_hbm.at[r], abuf.at[r], sems.at[2 * k + 1]),
            )
        )

    def fetch(k):
        if k < CHUNKS:
            for copy in copies[k]:
                copy.start()

    def prepare(k):
        if k < CHUNKS:
            for copy in copies[k]:
                copy.wait()
            fetch(k + DEPTH)
            r = slice(k * tile, k * tile + tile)
            gh[k % 2], gl[k % 2] = split(gbuf[r, :])
            ah[k % 2], al[k % 2] = split(abuf[r, :])

    for k in range(DEPTH):
        fetch(k)
    prepare(0)
    for k in range(CHUNKS):
        prepare(k + 1)
        now = k % 2
        for j in range(0, cin, 256):
            c = slice(j, j + 256)
            part = gram3(ah[now, :, c], al[now, :, c], gh[now], gl[now])
            grad[c, :] = part if k == 0 else grad[c, :] + part
        part = gram3(gh[now], gl[now], gh[now], gl[now])
        small[...] = part if k == 0 else small[...] + part

    core = core_ref[0]
    for which, out in ((core, mine_ref), (1 - core, other_ref)):
        for q in range(8):
            owner = 2 * q + which
            own = pl.ds(pl.multiple_of(owner * 64, 64), 64)
            for half in range(2):
                cols = slice(half * 128, half * 128 + 128)
                place = slice(half * 8, half * 8 + 8)
                out[q * 8 : q * 8 + 8, place, :] = grad[own, cols].reshape(8, 8, 128)
            for y in range(4):
                srows = pl.ds(pl.multiple_of(owner * 16 + 8 * (y // 2), 8), 8)
                part = small[srows, 128 * (y % 2) : 128 * (y % 2) + 128]
                out[q * 8 + 2 * y, 16:24, :] = part
                out[q * 8 + 2 * y + 1, 16:24, :] = part


def grad_parts(core, activations, out_grads):
    rows, cin = activations.shape
    cout = out_grads.shape[1]
    tile = rows // CHUNKS
    shape = jax.ShapeDtypeStruct((64, 24, 128), F32)
    return pl.pallas_call(
        grad_kernel,
        in_specs=[in_smem(), in_hbm(), in_hbm()],
        out_specs=[in_vmem()] * 2,
        out_shape=[shape, shape],
        scratch_shapes=[
            pltpu.VMEM((rows, cin), F32),
            pltpu.VMEM((rows, cout), F32),
            pltpu.VMEM((2, tile, cin), BF16),
            pltpu.VMEM((2, tile, cin), BF16),
            pltpu.VMEM((2, tile, cout), BF16),
            pltpu.VMEM((2, tile, cout), BF16),
            pltpu.VMEM((cin, cout), F32),
            pltpu.VMEM((cout, cout), F32),
            pltpu.SemaphoreType.DMA((2 * CHUNKS,)),
        ],
        compiler_params=pltpu.CompilerParams(vmem_limit_bytes=56 * 2**20),
        cost_estimate=pl.CostEstimate(flops=6 * rows * (cin + cout) * cout, bytes_accessed=4 * rows * (cin + cout), transcendentals=0),
        name="grad_parts",
    )(core, activations, out_grads)


def stat_kernel(core_ref, a_hbm, mine_ref, other_ref, buf, ah, al, acc, sems):
    cin = acc.shape[0]
    count = cin // 256
    copies = [
        pltpu.make_async_copy(a_hbm.at[:, j * 256 : j * 256 + 256], buf.at[j], sems.at[j]) for j in range(count)
    ]

    def prepare(j):
        if j < count:
            copies[j].wait()
            if j + DEPTH < count:
                copies[j + DEPTH].start()
            cj = slice(j * 256, j * 256 + 256)
            ah[:, cj], al[:, cj] = split(buf[j])

    for copy in copies[:DEPTH]:
        copy.start()
    prepare(0)
    for j in range(count):
        prepare(j + 1)
        cj = slice(j * 256, j * 256 + 256)
        for i in range(j + 1):
            ci = slice(i * 256, i * 256 + 256)
            acc[ci, cj] = gram3(ah[:, ci], al[:, ci], ah[:, cj], al[:, cj])
            if i < j:
                acc[cj, ci] = acc[ci, cj].T
    core = core_ref[0]
    for which, out in ((core, mine_ref), (1 - core, other_ref)):
        for q in range(8):
            own = pl.ds(pl.multiple_of((2 * q + which) * 64, 64), 64)
            for t in range(8):
                part = acc[own, 128 * t : 128 * t + 128]
                out[q * 8 : q * 8 + 8, 8 * t : 8 * t + 8, :] = part.reshape(8, 8, 128)


def stat_parts(core, activations):
    rows, cin = activations.shape
    shape = jax.ShapeDtypeStruct((64, 64, 128), F32)
    return pl.pallas_call(
        stat_kernel,
        in_specs=[in_smem(), in_hbm()],
        out_specs=[in_vmem()] * 2,
        out_shape=[shape, shape],
        scratch_shapes=[
            pltpu.VMEM((cin // 256, rows, 256), F32),
            pltpu.VMEM((rows, cin), BF16),
            pltpu.VMEM((rows, cin), BF16),
            pltpu.VMEM((cin, cin), F32),
            pltpu.SemaphoreType.DMA((cin // 256,)),
        ],
        compiler_params=pltpu.CompilerParams(vmem_limit_bytes=52 * 2**20),
        cost_estimate=pl.CostEstimate(flops=4 * rows * cin * cin, bytes_accessed=4 * rows * cin, transcendentals=0),
        name="stat_parts",
    )(core, activations)


def pack_kernel(mine_ref, got_ref, tail_ref, out_ref):
    lead = mine_ref.shape[1]
    out_ref[:, :lead, :] = mine_ref[...] + got_ref[...]
    for i in range(out_ref.shape[0]):
        out_ref[i, lead:, :] = tail_ref[...]


def pack(mine, got, tail, name):
    chunks, lead, lanes = mine.shape
    extra = tail.shape[0]
    spec = pl.BlockSpec((chunks // 4, lead, lanes), lambda i: (i, 0, 0))
    return pl.pallas_call(
        pack_kernel,
        grid=(4,),
        in_specs=[spec, spec, pl.BlockSpec((extra, lanes), lambda i: (0, 0))],
        out_specs=pl.BlockSpec((chunks // 4, lead + extra, lanes), lambda i: (i, 0, 0)),
        out_shape=jax.ShapeDtypeStruct((chunks, lead + extra, lanes), F32),
        compiler_params=pltpu.CompilerParams(vmem_limit_bytes=16 * 2**20),
        name=name,
    )(mine, got, tail)


def spread_kernel(all_ref, tile_ref, out_ref):
    total = jnp.sum(all_ref[:, :64, :], axis=0)
    for r in range(8):
        out_ref[r, :64, :] = total
        out_ref[r, 64:, :] = tile_ref[...]


def spread(parts, tile):
    return pl.pallas_call(
        spread_kernel,
        out_shape=jax.ShapeDtypeStruct((8, 72, 128), F32),
        compiler_params=pltpu.CompilerParams(vmem_limit_bytes=16 * 2**20),
        name="spread",
    )(parts, tile)


def blend_kernel(rows_ref, fa_ref, fg_ref, na_ref, ng_ref, *, total_rows):
    keep, fresh = decay_rate, 1.0 - decay_rate
    for t in range(8):
        cols = slice(128 * t, 128 * t + 128)
        stat = rows_ref[:, 8 * t : 8 * t + 8, :].reshape(64, 128) / total_rows
        na_ref[:, cols] = keep * fa_ref[:, cols] + fresh * stat
    for y in range(4):
        r, c = slice(8 * (y // 2), 8 * (y // 2) + 8), slice(128 * (y % 2), 128 * (y % 2) + 128)
        ng_ref[r, c] = keep * fg_ref[r, c] + fresh * rows_ref[2 * y, 64:72, :]


def blend(rows, factor_a, factor_g, total_rows):
    return pl.pallas_call(
        lambda *refs: blend_kernel(*refs, total_rows=total_rows),
        out_shape=[jax.ShapeDtypeStruct(factor_a.shape, F32), jax.ShapeDtypeStruct(factor_g.shape, F32)],
        name="blend",
    )(rows, factor_a, factor_g)


def final_kernel(core_ref, inv_a_ref, own_ref, got_ref, inv_own_ref, inv_got_ref, out_ref, grad, inv_g):
    core = core_ref[0]
    for which, part, inv in ((core, own_ref, inv_own_ref), (1 - core, got_ref, inv_got_ref)):
        for q in range(8):
            owner = 2 * q + which
            rows = pl.ds(pl.multiple_of(owner * 64, 64), 64)
            for half in range(2):
                block = part[q * 8 : q * 8 + 8, half * 8 : half * 8 + 8, :]
                grad[rows, half * 128 : half * 128 + 128] = block.reshape(64, 128)
            for y in range(4):
                rows = pl.ds(pl.multiple_of(owner * 16 + 8 * (y // 2), 8), 8)
                inv_g[rows, 128 * (y % 2) : 128 * (y % 2) + 128] = inv[q * 8 + 2 * y]
    high = lax.Precision.HIGHEST
    left = jnp.dot(inv_a_ref[...], grad[...], precision=high, preferred_element_type=F32)
    out_ref[...] = jnp.dot(left, inv_g[...], precision=high, preferred_element_type=F32)


def final(core, inverse_a, own, got, inv_own, inv_got):
    cout = 256
    return pl.pallas_call(
        final_kernel,
        in_specs=[in_smem()] + [in_vmem()] * 5,
        out_specs=in_vmem(),
        out_shape=jax.ShapeDtypeStruct((inverse_a.shape[0], cout), F32),
        scratch_shapes=[pltpu.VMEM((inverse_a.shape[1], cout), F32), pltpu.VMEM((cout, cout), F32)],
        compiler_params=pltpu.CompilerParams(vmem_limit_bytes=16 * 2**20),
        name="final",
    )(core, inverse_a, own, got, inv_own, inv_got)


def twin(flat):
    return (flat // 16) * 16 + (flat + 8) % 16


def swap(array):
    return lax.ppermute(array, SUB, [(i, twin(i)) for i in range(128)])


def exchange(array, axes):
    return lax.all_to_all(array, axes, 0, 0, tiled=True)


def local(activations, out_grads, factor_a, factor_g, inverse_a, inverse_g):
    total_rows = activations.shape[0] * 128
    core = lax.axis_index("co").astype(jnp.int32).reshape(1)
    y = lax.axis_index("y")

    g_mine, g_other = grad_parts(core, activations, out_grads)
    tile = lax.dynamic_slice(inverse_g, (8 * (y // 2), 128 * (y % 2)), (8, 128))
    g_sum = pack(g_mine, swap(g_other), tile, "grad_sum")
    g_sum, core = lax.optimization_barrier((g_sum, core))
    g_all = exchange(g_sum, CHIPS)

    s_mine, s_other = stat_parts(core, activations)
    g_all, s_mine, s_other = lax.optimization_barrier((g_all, s_mine, s_other))
    g_own = jnp.sum(g_all[:, :24], axis=0)
    inv_own = g_all[:, 24:]
    s_sum = pack(s_mine, swap(s_other), g_own[:16], "stat_sum")
    s_all = exchange(s_sum, CHIPS)
    inv_got = swap(inv_own)

    own = s_all[:, 64:]
    got = swap(own)
    rows = exchange(spread(s_all, g_own[16:]), ("y", "zh"))
    precond_grad = final(core, inverse_a, own, got, inv_own, inv_got)
    rows, precond_grad = lax.optimization_barrier((rows, precond_grad))
    new_factor_a, new_factor_g = blend(rows, factor_a, factor_g, total_rows)
    return new_factor_a, new_factor_g, precond_grad


def solution(mesh):
    fine = jax.sharding.Mesh(mesh.devices.reshape(SIZES), SUB)
    rows = P(SUB, None)
    panel = P(("x", "zl", "co"), None)
    return jax.shard_map(
        local,
        mesh=fine,
        in_specs=(rows, rows, panel, panel, panel, panel),
        out_specs=(panel, panel, panel),
        check_vma=False,
    )
```

```python
import jax
import jax.numpy as jnp
from jax import lax
from jax.experimental import pallas as pl
from jax.experimental.pallas import tpu as pltpu
from jax.sharding import PartitionSpec as P

decay_rate = 0.6
F32 = jnp.float32
BF16 = jnp.bfloat16
SUB = ("x", "zl", "co", "y", "zh")
SIZES = (4, 2, 2, 4, 2)
CHIPS = ("x", "zl", "y", "zh")
CHUNKS = 6
DEPTH = 2


def split(block):
    high = block.astype(BF16)
    return high, (block - high.astype(F32)).astype(BF16)


def gram(left, right):
    return lax.dot_general(left, right, (((0,), (0,)), ((), ())), preferred_element_type=F32)


def gram3(lh, ll, rh, rl):
    return gram(lh, rh) + gram(lh, rl) + gram(ll, rh)


def in_hbm():
    return pl.BlockSpec(memory_space=pltpu.HBM)


def in_vmem():
    return pl.BlockSpec(memory_space=pltpu.VMEM)


def in_smem():
    return pl.BlockSpec(memory_space=pltpu.SMEM)


def grad_kernel(core_ref, a_hbm, g_hbm, mine_ref, other_ref, abuf, gbuf, grad, small, sems):
    rows, cin = abuf.shape
    tile = rows // CHUNKS
    copies = []
    for k in range(CHUNKS):
        r = slice(k * tile, k * tile + tile)
        copies.append(
            (
                pltpu.make_async_copy(g_hbm.at[r], gbuf.at[r], sems.at[2 * k]),
                pltpu.make_async_copy(a_hbm.at[r], abuf.at[r], sems.at[2 * k + 1]),
            )
        )

    for k in range(DEPTH):
        for copy in copies[k]:
            copy.start()
    for k in range(CHUNKS):
        for copy in copies[k]:
            copy.wait()
        if k + DEPTH < CHUNKS:
            for copy in copies[k + DEPTH]:
                copy.start()
        r = slice(k * tile, k * tile + tile)
        gh, gl = split(gbuf[r, :])
        ah, al = split(abuf[r, :])
        for j in range(0, cin, 256):
            c = slice(j, j + 256)
            part = gram3(ah[:, c], al[:, c], gh, gl)
            grad[c, :] = part if k == 0 else grad[c, :] + part
        part = gram3(gh, gl, gh, gl)
        small[...] = part if k == 0 else small[...] + part

    core = core_ref[0]
    for which, out in ((core, mine_ref), (1 - core, other_ref)):
        for q in range(8):
            owner = 2 * q + which
            own = pl.ds(pl.multiple_of(owner * 64, 64), 64)
            for half in range(2):
                cols = slice(half * 128, half * 128 + 128)
                place = slice(half * 8, half * 8 + 8)
                out[q * 8 : q * 8 + 8, place, :] = grad[own, cols].reshape(8, 8, 128)
            for y in range(4):
                srows = pl.ds(pl.multiple_of(owner * 16 + 8 * (y // 2), 8), 8)
                part = small[srows, 128 * (y % 2) : 128 * (y % 2) + 128]
                out[q * 8 + 2 * y, 16:24, :] = part
                out[q * 8 + 2 * y + 1, 16:24, :] = part


def grad_parts(core, activations, out_grads):
    rows, cin = activations.shape
    cout = out_grads.shape[1]
    shape = jax.ShapeDtypeStruct((64, 24, 128), F32)
    return pl.pallas_call(
        grad_kernel,
        in_specs=[in_smem(), in_hbm(), in_hbm()],
        out_specs=[in_vmem()] * 2,
        out_shape=[shape, shape],
        scratch_shapes=[
            pltpu.VMEM((rows, cin), F32),
            pltpu.VMEM((rows, cout), F32),
            pltpu.VMEM((cin, cout), F32),
            pltpu.VMEM((cout, cout), F32),
            pltpu.SemaphoreType.DMA((2 * CHUNKS,)),
        ],
        compiler_params=pltpu.CompilerParams(vmem_limit_bytes=56 * 2**20),
        cost_estimate=pl.CostEstimate(flops=6 * rows * (cin + cout) * cout, bytes_accessed=4 * rows * (cin + cout), transcendentals=0),
        name="grad_parts",
    )(core, activations, out_grads)


def stat_kernel(core_ref, a_hbm, mine_ref, other_ref, buf, ah, al, acc, sems):
    cin = acc.shape[0]
    count = cin // 256
    copies = [
        pltpu.make_async_copy(a_hbm.at[:, j * 256 : j * 256 + 256], buf.at[j], sems.at[j]) for j in range(count)
    ]

    for copy in copies[:DEPTH]:
        copy.start()
    for j in range(count):
        copies[j].wait()
        if j + DEPTH < count:
            copies[j + DEPTH].start()
        cj = slice(j * 256, j * 256 + 256)
        ah[:, cj], al[:, cj] = split(buf[j])
        for i in range(j + 1):
            ci = slice(i * 256, i * 256 + 256)
            acc[ci, cj] = gram3(ah[:, ci], al[:, ci], ah[:, cj], al[:, cj])
            if i < j:
                acc[cj, ci] = acc[ci, cj].T

    low = lax.broadcasted_iota(jnp.int32, (32, 128), 1) < 64
    for side in range(2):

        @pl.when(core_ref[0] == side)
        def _():
            for p in range(16):
                out = mine_ref if p % 2 == side else other_ref
                for r in range(8):
                    place = p // 2 * 8 + r
                    c = (p + r) % 16
                    block = acc[64 * p : 64 * p + 64, c // 2 * 128 : c // 2 * 128 + 128]
                    top, bottom = block[:32], block[32:]
                    if c % 2 == 0:
                        bottom = pltpu.roll(bottom, 64, 1)
                    else:
                        top = pltpu.roll(top, 64, 1)
                    out[place, :32, :] = jnp.where(low, top, bottom)
                    far = (p + 8) % 16 // 2 * 128
                    out[place, 32:, :] = acc[64 * p + 8 * r : 64 * p + 8 * r + 8, far : far + 128]


def stat_parts(core, activations):
    rows, cin = activations.shape
    shape = jax.ShapeDtypeStruct((64, 40, 128), F32)
    return pl.pallas_call(
        stat_kernel,
        in_specs=[in_smem(), in_hbm()],
        out_specs=[in_vmem()] * 2,
        out_shape=[shape, shape],
        scratch_shapes=[
            pltpu.VMEM((cin // 256, rows, 256), F32),
            pltpu.VMEM((rows, cin), BF16),
            pltpu.VMEM((rows, cin), BF16),
            pltpu.VMEM((cin, cin), F32),
            pltpu.SemaphoreType.DMA((cin // 256,)),
        ],
        compiler_params=pltpu.CompilerParams(vmem_limit_bytes=52 * 2**20),
        cost_estimate=pl.CostEstimate(flops=4 * rows * cin * cin, bytes_accessed=4 * rows * cin, transcendentals=0),
        name="stat_parts",
    )(core, activations)


def pack_kernel(mine_ref, got_ref, tail_ref, out_ref):
    lead = mine_ref.shape[1]
    out_ref[:, :lead, :] = mine_ref[...] + got_ref[...]
    for i in range(out_ref.shape[0]):
        out_ref[i, lead:, :] = tail_ref[...]


def pack(mine, got, tail, name):
    chunks, lead, lanes = mine.shape
    extra = tail.shape[0]
    spec = pl.BlockSpec((chunks // 4, lead, lanes), lambda i: (i, 0, 0))
    return pl.pallas_call(
        pack_kernel,
        grid=(4,),
        in_specs=[spec, spec, pl.BlockSpec((extra, lanes), lambda i: (0, 0))],
        out_specs=pl.BlockSpec((chunks // 4, lead + extra, lanes), lambda i: (i, 0, 0)),
        out_shape=jax.ShapeDtypeStruct((chunks, lead + extra, lanes), F32),
        compiler_params=pltpu.CompilerParams(vmem_limit_bytes=16 * 2**20),
        name=name,
    )(mine, got, tail)


def spread_kernel(near_ref, mirror_ref, tile_ref, out_ref):
    for r in range(8):
        out_ref[r, :32, :] = near_ref[:32, :]
        out_ref[r, 32:64, :] = mirror_ref[...]
        out_ref[r, 64:72, :] = near_ref[32:40, :]
        out_ref[r, 72:, :] = tile_ref[...]


def spread(near, mirror, tile):
    return pl.pallas_call(
        spread_kernel,
        out_shape=jax.ShapeDtypeStruct((8, 80, 128), F32),
        name="spread",
    )(near, mirror, tile)


def blend_kernel(place_ref, rows_ref, fa_ref, fg_ref, na_ref, ng_ref, stat, *, total_rows):
    keep, fresh = decay_rate, 1.0 - decay_rate
    panel = place_ref[1]
    for c in range(16):
        cols = slice(64 * c, 64 * c + 64)
        k = (c - panel + 16) % 16

        @pl.when(k < 8)
        def _():
            block = rows_ref[k, :32, :]
            stat[:32, cols] = block[:, :64]
            stat[32:, cols] = block[:, 64:]

        @pl.when(k == 8)
        def _():
            half = 64 * (c % 2)
            stat[:, cols] = rows_ref[:, 64:72, :].reshape(64, 128)[:, half : half + 64]

        @pl.when(k > 8)
        def _():
            turned = rows_ref[16 - k, 32:64, :].T
            stat[:, 64 * c : 64 * c + 32] = turned[:64]
            stat[:, 64 * c + 32 : 64 * c + 64] = turned[64:]

    na_ref[...] = keep * fa_ref[...] + fresh * (stat[...] / total_rows)
    for y in range(4):
        r, c = slice(8 * (y // 2), 8 * (y // 2) + 8), slice(128 * (y % 2), 128 * (y % 2) + 128)
        ng_ref[r, c] = keep * fg_ref[r, c] + fresh * rows_ref[2 * y, 72:80, :]


def blend(place, rows, factor_a, factor_g, total_rows):
    return pl.pallas_call(
        lambda *refs: blend_kernel(*refs, total_rows=total_rows),
        in_specs=[in_smem()] + [in_vmem()] * 3,
        out_specs=[in_vmem()] * 2,
        out_shape=[jax.ShapeDtypeStruct(factor_a.shape, F32), jax.ShapeDtypeStruct(factor_g.shape, F32)],
        scratch_shapes=[pltpu.VMEM(factor_a.shape, F32)],
        name="blend",
    )(place, rows, factor_a, factor_g)


def final_kernel(core_ref, inv_a_ref, own_ref, got_ref, inv_own_ref, inv_got_ref, out_ref, grad, inv_g):
    core = core_ref[0]
    for which, part, inv in ((core, own_ref, inv_own_ref), (1 - core, got_ref, inv_got_ref)):
        for q in range(8):
            owner = 2 * q + which
            rows = pl.ds(pl.multiple_of(owner * 64, 64), 64)
            for half in range(2):
                block = part[q * 8 : q * 8 + 8, half * 8 : half * 8 + 8, :]
                grad[rows, half * 128 : half * 128 + 128] = block.reshape(64, 128)
            for y in range(4):
                rows = pl.ds(pl.multiple_of(owner * 16 + 8 * (y // 2), 8), 8)
                inv_g[rows, 128 * (y % 2) : 128 * (y % 2) + 128] = inv[q * 8 + 2 * y]
    high = lax.Precision.HIGHEST
    left = jnp.dot(inv_a_ref[...], grad[...], precision=high, preferred_element_type=F32)
    out_ref[...] = jnp.dot(left, inv_g[...], precision=high, preferred_element_type=F32)


def final(core, inverse_a, own, got, inv_own, inv_got):
    cout = 256
    return pl.pallas_call(
        final_kernel,
        in_specs=[in_smem()] + [in_vmem()] * 5,
        out_specs=in_vmem(),
        out_shape=jax.ShapeDtypeStruct((inverse_a.shape[0], cout), F32),
        scratch_shapes=[pltpu.VMEM((inverse_a.shape[1], cout), F32), pltpu.VMEM((cout, cout), F32)],
        compiler_params=pltpu.CompilerParams(vmem_limit_bytes=16 * 2**20),
        name="final",
    )(core, inverse_a, own, got, inv_own, inv_got)


def twin(flat):
    return (flat // 16) * 16 + (flat + 8) % 16


def across(flat):
    panel, rep = flat // 8, flat % 8
    return (panel + rep) % 16 * 8 + rep


def swap(array, to=twin):
    return lax.ppermute(array, SUB, [(i, to(i)) for i in range(128)])


def exchange(array, axes):
    return lax.all_to_all(array, axes, 0, 0, tiled=True)


def local(activations, out_grads, factor_a, factor_g, inverse_a, inverse_g):
    total_rows = activations.shape[0] * 128
    core = jnp.stack([lax.axis_index("co"), lax.axis_index(("x", "zl", "co"))]).astype(jnp.int32)
    y = lax.axis_index("y")

    g_mine, g_other = grad_parts(core, activations, out_grads)
    tile = lax.dynamic_slice(inverse_g, (8 * (y // 2), 128 * (y % 2)), (8, 128))
    g_sum = pack(g_mine, swap(g_other), tile, "grad_sum")
    g_sum, core = lax.optimization_barrier((g_sum, core))
    g_all = exchange(g_sum, CHIPS)

    s_mine, s_other = stat_parts(core, activations)
    g_all, s_mine, s_other = lax.optimization_barrier((g_all, s_mine, s_other))
    g_own = jnp.sum(g_all[:, :24], axis=0)
    inv_own = g_all[:, 24:]
    s_sum = pack(s_mine, swap(s_other), g_own[:16], "stat_sum")
    s_all = exchange(s_sum, CHIPS)
    inv_got = swap(inv_own)

    near = jnp.sum(s_all[:, :40], axis=0)
    mirror = swap(near[:32], across)
    own = s_all[:, 40:]
    got = swap(own)
    rows = exchange(spread(near, mirror, g_own[16:]), ("y", "zh"))
    precond_grad = final(core, inverse_a, own, got, inv_own, inv_got)
    rows, precond_grad = lax.optimization_barrier((rows, precond_grad))
    new_factor_a, new_factor_g = blend(core, rows, factor_a, factor_g, total_rows)
    return new_factor_a, new_factor_g, precond_grad


def solution(mesh):
    fine = jax.sharding.Mesh(mesh.devices.reshape(SIZES), SUB)
    rows = P(SUB, None)
    panel = P(("x", "zl", "co"), None)
    return jax.shard_map(
        local,
        mesh=fine,
        in_specs=(rows, rows, panel, panel, panel, panel),
        out_specs=(panel, panel, panel),
        check_vma=False,
    )
```

```python
import jax
import jax.numpy as jnp
from jax import lax
from jax.experimental import pallas as pl
from jax.experimental.pallas import tpu as pltpu
from jax.sharding import PartitionSpec as P

decay_rate = 0.6
F32 = jnp.float32
BF16 = jnp.bfloat16
SUB = ("x", "zl", "co", "y", "zh")
SIZES = (4, 2, 2, 4, 2)
CHIPS = ("x", "zl", "y", "zh")
CHUNKS = 6
DEPTH = 2


def split(block):
    high = block.astype(BF16)
    return high, (block - high.astype(F32)).astype(BF16)


def gram(left, right):
    return lax.dot_general(left, right, (((0,), (0,)), ((), ())), preferred_element_type=F32)


def gram3(lh, ll, rh, rl):
    return gram(lh, rh) + gram(lh, rl) + gram(ll, rh)


def in_hbm():
    return pl.BlockSpec(memory_space=pltpu.HBM)


def in_vmem():
    return pl.BlockSpec(memory_space=pltpu.VMEM)


def in_smem():
    return pl.BlockSpec(memory_space=pltpu.SMEM)


def grad_kernel(core_ref, a_hbm, g_hbm, mine_ref, other_ref, abuf, gbuf, grad, small, sems):
    rows, cin = abuf.shape
    tile = rows // CHUNKS
    copies = []
    for k in range(CHUNKS):
        r = slice(k * tile, k * tile + tile)
        copies.append(
            (
                pltpu.make_async_copy(g_hbm.at[r], gbuf.at[r], sems.at[2 * k]),
                pltpu.make_async_copy(a_hbm.at[r], abuf.at[r], sems.at[2 * k + 1]),
            )
        )

    for k in range(DEPTH):
        for copy in copies[k]:
            copy.start()
    for k in range(CHUNKS):
        for copy in copies[k]:
            copy.wait()
        if k + DEPTH < CHUNKS:
            for copy in copies[k + DEPTH]:
                copy.start()

        @pl.when(core_ref[0] >= 0)
        def _(k=k):
            r = slice(k * tile, k * tile + tile)
            gh, gl = split(gbuf[r, :])
            ah, al = split(abuf[r, :])
            for j in range(0, cin, 256):
                c = slice(j, j + 256)
                part = gram3(ah[:, c], al[:, c], gh, gl)
                grad[c, :] = part if k == 0 else grad[c, :] + part
            part = gram3(gh, gl, gh, gl)
            small[...] = part if k == 0 else small[...] + part

    core = core_ref[0]
    for which, out in ((core, mine_ref), (1 - core, other_ref)):
        for q in range(8):
            owner = 2 * q + which
            own = pl.ds(pl.multiple_of(owner * 64, 64), 64)
            for half in range(2):
                cols = slice(half * 128, half * 128 + 128)
                place = slice(half * 8, half * 8 + 8)
                out[q * 8 : q * 8 + 8, place, :] = grad[own, cols].reshape(8, 8, 128)
            for y in range(4):
                srows = pl.ds(pl.multiple_of(owner * 16 + 8 * (y // 2), 8), 8)
                part = small[srows, 128 * (y % 2) : 128 * (y % 2) + 128]
                out[q * 8 + 2 * y, 16:24, :] = part
                out[q * 8 + 2 * y + 1, 16:24, :] = part


def grad_parts(core, activations, out_grads):
    rows, cin = activations.shape
    cout = out_grads.shape[1]
    shape = jax.ShapeDtypeStruct((64, 24, 128), F32)
    return pl.pallas_call(
        grad_kernel,
        in_specs=[in_smem(), in_hbm(), in_hbm()],
        out_specs=[in_vmem()] * 2,
        out_shape=[shape, shape],
        scratch_shapes=[
            pltpu.VMEM((rows, cin), F32),
            pltpu.VMEM((rows, cout), F32),
            pltpu.VMEM((cin, cout), F32),
            pltpu.VMEM((cout, cout), F32),
            pltpu.SemaphoreType.DMA((2 * CHUNKS,)),
        ],
        compiler_params=pltpu.CompilerParams(vmem_limit_bytes=56 * 2**20),
        cost_estimate=pl.CostEstimate(flops=6 * rows * (cin + cout) * cout, bytes_accessed=4 * rows * (cin + cout), transcendentals=0),
        name="grad_parts",
    )(core, activations, out_grads)


def stat_kernel(core_ref, a_hbm, mine_ref, other_ref, buf, ah, al, acc, sems):
    cin = acc.shape[0]
    count = cin // 256
    copies = [
        pltpu.make_async_copy(a_hbm.at[:, j * 256 : j * 256 + 256], buf.at[j], sems.at[j]) for j in range(count)
    ]

    for copy in copies[:1]:
        copy.start()
    for j in range(count):
        copies[j].wait()
        if j + 1 < count:
            copies[j + 1].start()

        @pl.when(core_ref[0] >= 0)
        def _(j=j):
            cj = slice(j * 256, j * 256 + 256)
            ah[:, cj], al[:, cj] = split(buf[j])
            for i in range(j + 1):
                ci = slice(i * 256, i * 256 + 256)
                acc[ci, cj] = gram3(ah[:, ci], al[:, ci], ah[:, cj], al[:, cj])
                if i < j:
                    acc[cj, ci] = acc[ci, cj].T

    low = lax.broadcasted_iota(jnp.int32, (32, 128), 1) < 64
    for side in range(2):

        @pl.when(core_ref[0] == side)
        def _():
            for p in range(16):
                out = mine_ref if p % 2 == side else other_ref
                for r in range(8):
                    place = p // 2 * 8 + r
                    c = (p + r) % 16
                    block = acc[64 * p : 64 * p + 64, c // 2 * 128 : c // 2 * 128 + 128]
                    top, bottom = block[:32], block[32:]
                    if c % 2 == 0:
                        bottom = pltpu.roll(bottom, 64, 1)
                    else:
                        top = pltpu.roll(top, 64, 1)
                    out[place, :32, :] = jnp.where(low, top, bottom)
                    far = (p + 8) % 16 // 2 * 128
                    out[place, 32:, :] = acc[64 * p + 8 * r : 64 * p + 8 * r + 8, far : far + 128]


def stat_parts(core, activations):
    rows, cin = activations.shape
    shape = jax.ShapeDtypeStruct((64, 40, 128), F32)
    return pl.pallas_call(
        stat_kernel,
        in_specs=[in_smem(), in_hbm()],
        out_specs=[in_vmem()] * 2,
        out_shape=[shape, shape],
        scratch_shapes=[
            pltpu.VMEM((cin // 256, rows, 256), F32),
            pltpu.VMEM((rows, cin), BF16),
            pltpu.VMEM((rows, cin), BF16),
            pltpu.VMEM((cin, cin), F32),
            pltpu.SemaphoreType.DMA((cin // 256,)),
        ],
        compiler_params=pltpu.CompilerParams(vmem_limit_bytes=52 * 2**20),
        cost_estimate=pl.CostEstimate(flops=4 * rows * cin * cin, bytes_accessed=4 * rows * cin, transcendentals=0),
        name="stat_parts",
    )(core, activations)


def pack_kernel(mine_ref, got_ref, tail_ref, out_ref):
    lead = mine_ref.shape[1]
    out_ref[:, :lead, :] = mine_ref[...] + got_ref[...]
    extra = out_ref.shape[1] - lead
    for i in range(out_ref.shape[0]):
        out_ref[i, lead:, :] = tail_ref[:extra, :]


def pack(mine, got, tail, extra, name):
    chunks, lead, lanes = mine.shape
    spec = pl.BlockSpec((chunks // 4, lead, lanes), lambda i: (i, 0, 0))
    return pl.pallas_call(
        pack_kernel,
        grid=(4,),
        in_specs=[spec, spec, pl.BlockSpec(tail.shape, lambda i: (0, 0))],
        out_specs=pl.BlockSpec((chunks // 4, lead + extra, lanes), lambda i: (i, 0, 0)),
        out_shape=jax.ShapeDtypeStruct((chunks, lead + extra, lanes), F32),
        compiler_params=pltpu.CompilerParams(vmem_limit_bytes=16 * 2**20),
        name=name,
    )(mine, got, tail)


def spread_kernel(near_ref, mirror_ref, tile_ref, out_ref):
    for r in range(8):
        out_ref[r, :32, :] = near_ref[:32, :]
        out_ref[r, 32:64, :] = mirror_ref[...]
        out_ref[r, 64:72, :] = near_ref[32:40, :]
        out_ref[r, 72:, :] = tile_ref[16:, :]


def spread(near, mirror, tile):
    return pl.pallas_call(
        spread_kernel,
        out_shape=jax.ShapeDtypeStruct((8, 80, 128), F32),
        compiler_params=pltpu.CompilerParams(vmem_limit_bytes=16 * 2**20),
        name="spread",
    )(near, mirror, tile)


def blend_kernel(place_ref, rows_ref, fa_ref, fg_ref, na_ref, ng_ref, stat, *, total_rows):
    keep, fresh = decay_rate, 1.0 - decay_rate
    panel = place_ref[0]
    for c in range(16):
        cols = slice(64 * c, 64 * c + 64)
        k = (c - panel + 16) % 16

        @pl.when(k < 8)
        def _():
            block = rows_ref[k, :32, :]
            stat[:32, cols] = block[:, :64]
            stat[32:, cols] = block[:, 64:]

        @pl.when(k == 8)
        def _():
            half = 64 * (c % 2)
            stat[:, cols] = rows_ref[:, 64:72, :].reshape(64, 128)[:, half : half + 64]

        @pl.when(k > 8)
        def _():
            turned = rows_ref[16 - k, 32:64, :].T
            stat[:, 64 * c : 64 * c + 32] = turned[:64]
            stat[:, 64 * c + 32 : 64 * c + 64] = turned[64:]

    na_ref[...] = keep * fa_ref[...] + fresh * (stat[...] / total_rows)
    for y in range(4):
        r, c = slice(8 * (y // 2), 8 * (y // 2) + 8), slice(128 * (y % 2), 128 * (y % 2) + 128)
        ng_ref[r, c] = keep * fg_ref[r, c] + fresh * rows_ref[2 * y, 72:80, :]


def blend(place, rows, factor_a, factor_g, total_rows):
    return pl.pallas_call(
        lambda *refs: blend_kernel(*refs, total_rows=total_rows),
        in_specs=[in_smem()] + [in_vmem()] * 3,
        out_specs=[in_vmem()] * 2,
        out_shape=[jax.ShapeDtypeStruct(factor_a.shape, F32), jax.ShapeDtypeStruct(factor_g.shape, F32)],
        scratch_shapes=[pltpu.VMEM(factor_a.shape, F32)],
        compiler_params=pltpu.CompilerParams(vmem_limit_bytes=16 * 2**20),
        name="blend",
    )(place, rows, factor_a, factor_g)


def final_kernel(core_ref, inv_a_ref, own_ref, got_ref, inv_own_ref, inv_got_ref, out_ref, grad, inv_g):
    core = core_ref[0]
    for which, part, inv in ((core, own_ref, inv_own_ref), (1 - core, got_ref, inv_got_ref)):
        for q in range(8):
            owner = 2 * q + which
            rows = pl.ds(pl.multiple_of(owner * 64, 64), 64)
            for half in range(2):
                block = part[q * 8 : q * 8 + 8, half * 8 : half * 8 + 8, :]
                grad[rows, half * 128 : half * 128 + 128] = block.reshape(64, 128)
            for y in range(4):
                rows = pl.ds(pl.multiple_of(owner * 16 + 8 * (y // 2), 8), 8)
                inv_g[rows, 128 * (y % 2) : 128 * (y % 2) + 128] = inv[q * 8 + 2 * y]
    high = lax.Precision.HIGHEST
    left = jnp.dot(inv_a_ref[...], grad[...], precision=high, preferred_element_type=F32)
    out_ref[...] = jnp.dot(left, inv_g[...], precision=high, preferred_element_type=F32)


def final(core, inverse_a, own, got, inv_own, inv_got):
    cout = 256
    return pl.pallas_call(
        final_kernel,
        in_specs=[in_smem()] + [in_vmem()] * 5,
        out_specs=in_vmem(),
        out_shape=jax.ShapeDtypeStruct((inverse_a.shape[0], cout), F32),
        scratch_shapes=[pltpu.VMEM((inverse_a.shape[1], cout), F32), pltpu.VMEM((cout, cout), F32)],
        compiler_params=pltpu.CompilerParams(vmem_limit_bytes=16 * 2**20),
        name="final",
    )(core, inverse_a, own, got, inv_own, inv_got)


def twin(flat):
    return (flat // 16) * 16 + (flat + 8) % 16


def across(flat):
    panel, rep = flat // 8, flat % 8
    return (panel + rep) % 16 * 8 + rep


def swap(array, to=twin):
    return lax.ppermute(array, SUB, [(i, to(i)) for i in range(128)])


def exchange(array, axes):
    return lax.all_to_all(array, axes, 0, 0, tiled=True)


def local(activations, out_grads, factor_a, factor_g, inverse_a, inverse_g):
    total_rows = activations.shape[0] * 128
    core = lax.axis_index("co").astype(jnp.int32).reshape(1)
    place = lax.axis_index(("x", "zl", "co")).astype(jnp.int32).reshape(1)
    y = lax.axis_index("y")

    g_mine, g_other = grad_parts(core, activations, out_grads)
    tile = lax.dynamic_slice(inverse_g, (8 * (y // 2), 128 * (y % 2)), (8, 128))
    g_sum = pack(g_mine, swap(g_other), tile, 8, "grad_sum")
    g_sum, core = lax.optimization_barrier((g_sum, core))
    g_all = exchange(g_sum, CHIPS)

    s_mine, s_other = stat_parts(core, activations)
    g_all, s_mine, s_other = lax.optimization_barrier((g_all, s_mine, s_other))
    g_own = jnp.sum(g_all[:, :24], axis=0)
    inv_own = g_all[:, 24:]
    inv_got = swap(inv_own)
    s_sum = pack(s_mine, swap(s_other), g_own, 16, "stat_sum")
    s_sum, inv_got = lax.optimization_barrier((s_sum, inv_got))
    s_all = exchange(s_sum, CHIPS)

    near = jnp.sum(s_all[:, :40], axis=0)
    mirror = swap(near[:32], across)
    own = s_all[:, 40:]
    got = swap(own)
    rows = exchange(spread(near, mirror, g_own), ("y", "zh"))
    precond_grad = final(core, inverse_a, own, got, inv_own, inv_got)
    rows, precond_grad = lax.optimization_barrier((rows, precond_grad))
    new_factor_a, new_factor_g = blend(place, rows, factor_a, factor_g, total_rows)
    return new_factor_a, new_factor_g, precond_grad


def solution(mesh):
    fine = jax.sharding.Mesh(mesh.devices.reshape(SIZES), SUB)
    rows = P(SUB, None)
    panel = P(("x", "zl", "co"), None)
    return jax.shard_map(
        local,
        mesh=fine,
        in_specs=(rows, rows, panel, panel, panel, panel),
        out_specs=(panel, panel, panel),
        check_vma=False,
    )
```

```python
import jax
import jax.numpy as jnp
from jax import lax
from jax.experimental import pallas as pl
from jax.experimental.pallas import tpu as pltpu
from jax.sharding import PartitionSpec as P

decay_rate = 0.6
F32 = jnp.float32
BF16 = jnp.bfloat16
SUB = ("x", "zl", "co", "y", "zh")
SIZES = (4, 2, 2, 4, 2)
CHIPS = ("x", "zl", "y", "zh")
CHUNKS = 6
DEPTH = 2


def split(block):
    high = block.astype(BF16)
    return high, (block - high.astype(F32)).astype(BF16)


def gram(left, right):
    return lax.dot_general(left, right, (((0,), (0,)), ((), ())), preferred_element_type=F32)


def gram3(lh, ll, rh, rl):
    return gram(lh, rh) + gram(lh, rl) + gram(ll, rh)


def in_hbm():
    return pl.BlockSpec(memory_space=pltpu.HBM)


def in_vmem():
    return pl.BlockSpec(memory_space=pltpu.VMEM)


def in_smem():
    return pl.BlockSpec(memory_space=pltpu.SMEM)


def grad_kernel(core_ref, a_hbm, g_hbm, mine_ref, other_ref, abuf, gbuf, grad, small, sems):
    rows, cin = abuf.shape
    tile = rows // CHUNKS
    copies = []
    for k in range(CHUNKS):
        r = slice(k * tile, k * tile + tile)
        copies.append(
            (
                pltpu.make_async_copy(g_hbm.at[r], gbuf.at[r], sems.at[2 * k]),
                pltpu.make_async_copy(a_hbm.at[r], abuf.at[r], sems.at[2 * k + 1]),
            )
        )

    for k in range(DEPTH):
        for copy in copies[k]:
            copy.start()
    for k in range(CHUNKS):
        for copy in copies[k]:
            copy.wait()
        if k + DEPTH < CHUNKS:
            for copy in copies[k + DEPTH]:
                copy.start()

        @pl.when(core_ref[0] >= 0)
        def _(k=k):
            r = slice(k * tile, k * tile + tile)
            gh, gl = split(gbuf[r, :])
            ah, al = split(abuf[r, :])
            for j in range(0, cin, 256):
                c = slice(j, j + 256)
                part = gram3(ah[:, c], al[:, c], gh, gl)
                grad[c, :] = part if k == 0 else grad[c, :] + part
            part = gram3(gh, gl, gh, gl)
            small[...] = part if k == 0 else small[...] + part

    core = core_ref[0]
    for which, out in ((core, mine_ref), (1 - core, other_ref)):
        for q in range(8):
            owner = 2 * q + which
            own = pl.ds(pl.multiple_of(owner * 64, 64), 64)
            for half in range(2):
                cols = slice(half * 128, half * 128 + 128)
                place = slice(half * 8, half * 8 + 8)
                out[q * 8 : q * 8 + 8, place, :] = grad[own, cols].reshape(8, 8, 128)
            for y in range(4):
                srows = pl.ds(pl.multiple_of(owner * 16 + 8 * (y // 2), 8), 8)
                part = small[srows, 128 * (y % 2) : 128 * (y % 2) + 128]
                out[q * 8 + 2 * y, 16:24, :] = part
                out[q * 8 + 2 * y + 1, 16:24, :] = part


def grad_parts(core, activations, out_grads):
    rows, cin = activations.shape
    cout = out_grads.shape[1]
    shape = jax.ShapeDtypeStruct((64, 24, 128), F32)
    return pl.pallas_call(
        grad_kernel,
        in_specs=[in_smem(), in_hbm(), in_hbm()],
        out_specs=[in_vmem()] * 2,
        out_shape=[shape, shape],
        scratch_shapes=[
            pltpu.VMEM((rows, cin), F32),
            pltpu.VMEM((rows, cout), F32),
            pltpu.VMEM((cin, cout), F32),
            pltpu.VMEM((cout, cout), F32),
            pltpu.SemaphoreType.DMA((2 * CHUNKS,)),
        ],
        compiler_params=pltpu.CompilerParams(vmem_limit_bytes=56 * 2**20),
        cost_estimate=pl.CostEstimate(flops=6 * rows * (cin + cout) * cout, bytes_accessed=4 * rows * (cin + cout), transcendentals=0),
        name="grad_parts",
    )(core, activations, out_grads)


def stat_kernel(core_ref, a_hbm, mine_ref, other_ref, buf, ah, al, acc, cross, sems):
    cin = acc.shape[0]
    count = cin // 256
    copies = [
        pltpu.make_async_copy(a_hbm.at[:, j * 256 : j * 256 + 256], buf.at[j], sems.at[j]) for j in range(count)
    ]

    for copy in copies[:1]:
        copy.start()
    for j in range(count):
        copies[j].wait()
        if j + 1 < count:
            copies[j + 1].start()

        @pl.when(core_ref[0] >= 0)
        def _(j=j):
            cj = slice(j * 256, j * 256 + 256)
            ah[:, cj], al[:, cj] = split(buf[j])
            cross[j] = gram(ah[:, cj], al[:, cj])
            acc[cj, cj] = gram(ah[:, cj], ah[:, cj])
            for i in range(j):
                ci = slice(i * 256, i * 256 + 256)
                acc[ci, cj] = gram3(ah[:, ci], al[:, ci], ah[:, cj], al[:, cj])
                acc[cj, ci] = acc[ci, cj].T

    @pl.when(core_ref[0] >= 0)
    def _():
        for j in range(count):
            cj = slice(j * 256, j * 256 + 256)
            acc[cj, cj] = acc[cj, cj] + (cross[j] + cross[j].T)

    low = lax.broadcasted_iota(jnp.int32, (32, 128), 1) < 64
    for side in range(2):

        @pl.when(core_ref[0] == side)
        def _():
            for p in range(16):
                out = mine_ref if p % 2 == side else other_ref
                for r in range(8):
                    place = p // 2 * 8 + r
                    c = (p + r) % 16
                    block = acc[64 * p : 64 * p + 64, c // 2 * 128 : c // 2 * 128 + 128]
                    top, bottom = block[:32], block[32:]
                    if c % 2 == 0:
                        bottom = pltpu.roll(bottom, 64, 1)
                    else:
                        top = pltpu.roll(top, 64, 1)
                    out[place, :32, :] = jnp.where(low, top, bottom)
                    far = (p + 8) % 16 // 2 * 128
                    out[place, 32:, :] = acc[64 * p + 8 * r : 64 * p + 8 * r + 8, far : far + 128]


def stat_parts(core, activations):
    rows, cin = activations.shape
    shape = jax.ShapeDtypeStruct((64, 40, 128), F32)
    return pl.pallas_call(
        stat_kernel,
        in_specs=[in_smem(), in_hbm()],
        out_specs=[in_vmem()] * 2,
        out_shape=[shape, shape],
        scratch_shapes=[
            pltpu.VMEM((cin // 256, rows, 256), F32),
            pltpu.VMEM((rows, cin), BF16),
            pltpu.VMEM((rows, cin), BF16),
            pltpu.VMEM((cin, cin), F32),
            pltpu.VMEM((cin // 256, 256, 256), F32),
            pltpu.SemaphoreType.DMA((cin // 256,)),
        ],
        compiler_params=pltpu.CompilerParams(vmem_limit_bytes=52 * 2**20),
        cost_estimate=pl.CostEstimate(flops=4 * rows * cin * cin, bytes_accessed=4 * rows * cin, transcendentals=0),
        name="stat_parts",
    )(core, activations)


def pack_kernel(mine_ref, got_ref, tail_ref, out_ref):
    lead = mine_ref.shape[1]
    out_ref[:, :lead, :] = mine_ref[...] + got_ref[...]
    extra = out_ref.shape[1] - lead
    for i in range(out_ref.shape[0]):
        out_ref[i, lead:, :] = tail_ref[:extra, :]


def pack(mine, got, tail, extra, name):
    chunks, lead, lanes = mine.shape
    spec = pl.BlockSpec((chunks // 4, lead, lanes), lambda i: (i, 0, 0))
    return pl.pallas_call(
        pack_kernel,
        grid=(4,),
        in_specs=[spec, spec, pl.BlockSpec(tail.shape, lambda i: (0, 0))],
        out_specs=pl.BlockSpec((chunks // 4, lead + extra, lanes), lambda i: (i, 0, 0)),
        out_shape=jax.ShapeDtypeStruct((chunks, lead + extra, lanes), F32),
        compiler_params=pltpu.CompilerParams(vmem_limit_bytes=16 * 2**20),
        name=name,
    )(mine, got, tail)


def spread_kernel(near_ref, mirror_ref, tile_ref, out_ref):
    for r in range(8):
        out_ref[r, :32, :] = near_ref[:32, :]
        out_ref[r, 32:64, :] = mirror_ref[...]
        out_ref[r, 64:72, :] = near_ref[32:40, :]
        out_ref[r, 72:, :] = tile_ref[16:, :]


def spread(near, mirror, tile):
    return pl.pallas_call(
        spread_kernel,
        out_shape=jax.ShapeDtypeStruct((8, 80, 128), F32),
        compiler_params=pltpu.CompilerParams(vmem_limit_bytes=16 * 2**20),
        name="spread",
    )(near, mirror, tile)


def blend_kernel(place_ref, rows_ref, fa_ref, fg_ref, na_ref, ng_ref, stat, *, total_rows):
    keep, fresh = decay_rate, 1.0 - decay_rate
    panel = place_ref[0]
    for c in range(16):
        cols = slice(64 * c, 64 * c + 64)
        k = (c - panel + 16) % 16

        @pl.when(k < 8)
        def _():
            block = rows_ref[k, :32, :]
            stat[:32, cols] = block[:, :64]
            stat[32:, cols] = block[:, 64:]

        @pl.when(k == 8)
        def _():
            half = 64 * (c % 2)
            stat[:, cols] = rows_ref[:, 64:72, :].reshape(64, 128)[:, half : half + 64]

        @pl.when(k > 8)
        def _():
            turned = rows_ref[16 - k, 32:64, :].T
            stat[:, 64 * c : 64 * c + 32] = turned[:64]
            stat[:, 64 * c + 32 : 64 * c + 64] = turned[64:]

    na_ref[...] = keep * fa_ref[...] + fresh * (stat[...] / total_rows)
    for y in range(4):
        r, c = slice(8 * (y // 2), 8 * (y // 2) + 8), slice(128 * (y % 2), 128 * (y % 2) + 128)
        ng_ref[r, c] = keep * fg_ref[r, c] + fresh * rows_ref[2 * y, 72:80, :]


def blend(place, rows, factor_a, factor_g, total_rows):
    return pl.pallas_call(
        lambda *refs: blend_kernel(*refs, total_rows=total_rows),
        in_specs=[in_smem()] + [in_vmem()] * 3,
        out_specs=[in_vmem()] * 2,
        out_shape=[jax.ShapeDtypeStruct(factor_a.shape, F32), jax.ShapeDtypeStruct(factor_g.shape, F32)],
        scratch_shapes=[pltpu.VMEM(factor_a.shape, F32)],
        compiler_params=pltpu.CompilerParams(vmem_limit_bytes=16 * 2**20),
        name="blend",
    )(place, rows, factor_a, factor_g)


def final_kernel(core_ref, inv_a_ref, own_ref, got_ref, inv_own_ref, inv_got_ref, out_ref, grad, inv_g):
    core = core_ref[0]
    for which, part, inv in ((core, own_ref, inv_own_ref), (1 - core, got_ref, inv_got_ref)):
        for q in range(8):
            owner = 2 * q + which
            rows = pl.ds(pl.multiple_of(owner * 64, 64), 64)
            for half in range(2):
                block = part[q * 8 : q * 8 + 8, half * 8 : half * 8 + 8, :]
                grad[rows, half * 128 : half * 128 + 128] = block.reshape(64, 128)
            for y in range(4):
                rows = pl.ds(pl.multiple_of(owner * 16 + 8 * (y // 2), 8), 8)
                inv_g[rows, 128 * (y % 2) : 128 * (y % 2) + 128] = inv[q * 8 + 2 * y]
    high = lax.Precision.HIGHEST
    left = jnp.dot(inv_a_ref[...], grad[...], precision=high, preferred_element_type=F32)
    out_ref[...] = jnp.dot(left, inv_g[...], precision=high, preferred_element_type=F32)


def final(core, inverse_a, own, got, inv_own, inv_got):
    cout = 256
    return pl.pallas_call(
        final_kernel,
        in_specs=[in_smem()] + [in_vmem()] * 5,
        out_specs=in_vmem(),
        out_shape=jax.ShapeDtypeStruct((inverse_a.shape[0], cout), F32),
        scratch_shapes=[pltpu.VMEM((inverse_a.shape[1], cout), F32), pltpu.VMEM((cout, cout), F32)],
        compiler_params=pltpu.CompilerParams(vmem_limit_bytes=16 * 2**20),
        name="final",
    )(core, inverse_a, own, got, inv_own, inv_got)


def twin(flat):
    return (flat // 16) * 16 + (flat + 8) % 16


def across(flat):
    panel, rep = flat // 8, flat % 8
    return (panel + rep) % 16 * 8 + rep


def swap(array, to=twin):
    return lax.ppermute(array, SUB, [(i, to(i)) for i in range(128)])


def exchange(array, axes):
    return lax.all_to_all(array, axes, 0, 0, tiled=True)


def local(activations, out_grads, factor_a, factor_g, inverse_a, inverse_g):
    total_rows = activations.shape[0] * 128
    core = lax.axis_index("co").astype(jnp.int32).reshape(1)
    place = lax.axis_index(("x", "zl", "co")).astype(jnp.int32).reshape(1)
    y = lax.axis_index("y")

    g_mine, g_other = grad_parts(core, activations, out_grads)
    tile = lax.dynamic_slice(inverse_g, (8 * (y // 2), 128 * (y % 2)), (8, 128))
    g_sum = pack(g_mine, swap(g_other), tile, 8, "grad_sum")
    g_sum, core = lax.optimization_barrier((g_sum, core))
    g_all = exchange(g_sum, CHIPS)

    s_mine, s_other = stat_parts(core, activations)
    g_all, s_mine, s_other = lax.optimization_barrier((g_all, s_mine, s_other))
    g_own = jnp.sum(g_all[:, :24], axis=0)
    inv_own = g_all[:, 24:]
    inv_got = swap(inv_own)
    s_sum = pack(s_mine, swap(s_other), g_own, 16, "stat_sum")
    s_sum, inv_got = lax.optimization_barrier((s_sum, inv_got))
    s_all = exchange(s_sum, CHIPS)

    near = jnp.sum(s_all[:, :40], axis=0)
    mirror = swap(near[:32], across)
    own = s_all[:, 40:]
    got = swap(own)
    rows = exchange(spread(near, mirror, g_own), ("y", "zh"))
    precond_grad = final(core, inverse_a, own, got, inv_own, inv_got)
    rows, precond_grad = lax.optimization_barrier((rows, precond_grad))
    new_factor_a, new_factor_g = blend(place, rows, factor_a, factor_g, total_rows)
    return new_factor_a, new_factor_g, precond_grad


def solution(mesh):
    fine = jax.sharding.Mesh(mesh.devices.reshape(SIZES), SUB)
    rows = P(SUB, None)
    panel = P(("x", "zl", "co"), None)
    return jax.shard_map(
        local,
        mesh=fine,
        in_specs=(rows, rows, panel, panel, panel, panel),
        out_specs=(panel, panel, panel),
        check_vma=False,
    )
```

```python
import jax
import jax.numpy as jnp
from jax import lax
from jax.experimental import pallas as pl
from jax.experimental.pallas import tpu as pltpu
from jax.sharding import PartitionSpec as P

decay_rate = 0.6
F32 = jnp.float32
BF16 = jnp.bfloat16
SUB = ("x", "zl", "co", "y", "zh")
SIZES = (4, 2, 2, 4, 2)
CHIPS = ("x", "zl", "y", "zh")
CHUNKS = 6
DEPTH = 2


def split(block):
    high = block.astype(BF16)
    return high, (block - high.astype(F32)).astype(BF16)


def gram(left, right):
    return lax.dot_general(left, right, (((0,), (0,)), ((), ())), preferred_element_type=F32)


def gram3(lh, ll, rh, rl):
    return gram(lh, rh) + gram(lh, rl) + gram(ll, rh)


def in_hbm():
    return pl.BlockSpec(memory_space=pltpu.HBM)


def in_vmem():
    return pl.BlockSpec(memory_space=pltpu.VMEM)


def in_smem():
    return pl.BlockSpec(memory_space=pltpu.SMEM)


def grad_kernel(core_ref, a_hbm, g_hbm, mine_ref, other_ref, abuf, gbuf, grad, small, sems):
    rows, cin = abuf.shape
    tile = rows // CHUNKS
    copies = []
    for k in range(CHUNKS):
        r = slice(k * tile, k * tile + tile)
        copies.append(
            (
                pltpu.make_async_copy(g_hbm.at[r], gbuf.at[r], sems.at[2 * k]),
                pltpu.make_async_copy(a_hbm.at[r], abuf.at[r], sems.at[2 * k + 1]),
            )
        )

    for k in range(DEPTH):
        for copy in copies[k]:
            copy.start()
    for k in range(CHUNKS):
        for copy in copies[k]:
            copy.wait()
        if k + DEPTH < CHUNKS:
            for copy in copies[k + DEPTH]:
                copy.start()

        @pl.when(core_ref[0] >= 0)
        def _(k=k):
            r = slice(k * tile, k * tile + tile)
            gh, gl = split(gbuf[r, :])
            ah, al = split(abuf[r, :])
            for j in range(0, cin, 256):
                c = slice(j, j + 256)
                part = gram3(ah[:, c], al[:, c], gh, gl)
                grad[c, :] = part if k == 0 else grad[c, :] + part
            part = gram3(gh, gl, gh, gl)
            small[...] = part if k == 0 else small[...] + part

    core = core_ref[0]
    for which, out in ((core, mine_ref), (1 - core, other_ref)):
        for q in range(8):
            owner = 2 * q + which
            own = pl.ds(pl.multiple_of(owner * 64, 64), 64)
            for half in range(2):
                cols = slice(half * 128, half * 128 + 128)
                place = slice(half * 8, half * 8 + 8)
                out[q * 8 : q * 8 + 8, place, :] = grad[own, cols].reshape(8, 8, 128)
            for y in range(4):
                srows = pl.ds(pl.multiple_of(owner * 16 + 8 * (y // 2), 8), 8)
                part = small[srows, 128 * (y % 2) : 128 * (y % 2) + 128]
                out[q * 8 + 2 * y, 16:24, :] = part
                out[q * 8 + 2 * y + 1, 16:24, :] = part


def grad_parts(core, activations, out_grads):
    rows, cin = activations.shape
    cout = out_grads.shape[1]
    shape = jax.ShapeDtypeStruct((64, 24, 128), F32)
    return pl.pallas_call(
        grad_kernel,
        in_specs=[in_smem(), in_hbm(), in_hbm()],
        out_specs=[in_vmem()] * 2,
        out_shape=[shape, shape],
        scratch_shapes=[
            pltpu.VMEM((rows, cin), F32),
            pltpu.VMEM((rows, cout), F32),
            pltpu.VMEM((cin, cout), F32),
            pltpu.VMEM((cout, cout), F32),
            pltpu.SemaphoreType.DMA((2 * CHUNKS,)),
        ],
        compiler_params=pltpu.CompilerParams(vmem_limit_bytes=56 * 2**20),
        cost_estimate=pl.CostEstimate(flops=6 * rows * (cin + cout) * cout, bytes_accessed=4 * rows * (cin + cout), transcendentals=0),
        name="grad_parts",
    )(core, activations, out_grads)


def stat_kernel(core_ref, a_hbm, mine_ref, other_ref, buf, ah, al, acc, cross, sems):
    cin = acc.shape[0]
    count = cin // 256
    copies = [
        pltpu.make_async_copy(a_hbm.at[:, j * 256 : j * 256 + 256], buf.at[j], sems.at[j]) for j in range(count)
    ]

    for copy in copies[:1]:
        copy.start()
    for j in range(count):
        copies[j].wait()
        if j + 1 < count:
            copies[j + 1].start()

        @pl.when(core_ref[0] >= 0)
        def _(j=j):
            cj = slice(j * 256, j * 256 + 256)
            ah[:, cj], al[:, cj] = split(buf[j])
            cross[j] = gram(ah[:, cj], al[:, cj])
            acc[cj, cj] = gram(ah[:, cj], ah[:, cj])
            for i in range(j):
                ci = slice(i * 256, i * 256 + 256)
                acc[ci, cj] = gram3(ah[:, ci], al[:, ci], ah[:, cj], al[:, cj])
                acc[cj, ci] = acc[ci, cj].T

    @pl.when(core_ref[0] >= 0)
    def _():
        for j in range(count):
            cj = slice(j * 256, j * 256 + 256)
            acc[cj, cj] = acc[cj, cj] + (cross[j] + cross[j].T)

    low = lax.broadcasted_iota(jnp.int32, (32, 128), 1) < 64
    for side in range(2):

        @pl.when(core_ref[0] == side)
        def _():
            for p in range(16):
                out = mine_ref if p % 2 == side else other_ref
                for r in range(8):
                    place = p // 2 * 8 + r
                    c = (p + r) % 16
                    block = acc[64 * p : 64 * p + 64, c // 2 * 128 : c // 2 * 128 + 128]
                    top, bottom = block[:32], block[32:]
                    if c % 2 == 0:
                        bottom = pltpu.roll(bottom, 64, 1)
                    else:
                        top = pltpu.roll(top, 64, 1)
                    out[place, :32, :] = jnp.where(low, top, bottom)
                    far = (p + 8) % 16 // 2 * 128
                    out[place, 32:, :] = acc[64 * p + 8 * r : 64 * p + 8 * r + 8, far : far + 128]


def stat_parts(core, activations):
    rows, cin = activations.shape
    shape = jax.ShapeDtypeStruct((64, 40, 128), F32)
    return pl.pallas_call(
        stat_kernel,
        in_specs=[in_smem(), in_hbm()],
        out_specs=[in_vmem()] * 2,
        out_shape=[shape, shape],
        scratch_shapes=[
            pltpu.VMEM((cin // 256, rows, 256), F32),
            pltpu.VMEM((rows, cin), BF16),
            pltpu.VMEM((rows, cin), BF16),
            pltpu.VMEM((cin, cin), F32),
            pltpu.VMEM((cin // 256, 256, 256), F32),
            pltpu.SemaphoreType.DMA((cin // 256,)),
        ],
        compiler_params=pltpu.CompilerParams(vmem_limit_bytes=52 * 2**20),
        cost_estimate=pl.CostEstimate(flops=4 * rows * cin * cin, bytes_accessed=4 * rows * cin, transcendentals=0),
        name="stat_parts",
    )(core, activations)


def pack_kernel(mine_ref, got_ref, tail_ref, out_ref):
    lead = mine_ref.shape[1]
    out_ref[:, :lead, :] = mine_ref[...] + got_ref[...]
    extra = out_ref.shape[1] - lead
    for i in range(out_ref.shape[0]):
        out_ref[i, lead:, :] = tail_ref[:extra, :]


def pack(mine, got, tail, extra, name):
    chunks, lead, lanes = mine.shape
    spec = pl.BlockSpec((chunks // 4, lead, lanes), lambda i: (i, 0, 0))
    return pl.pallas_call(
        pack_kernel,
        grid=(4,),
        in_specs=[spec, spec, pl.BlockSpec(tail.shape, lambda i: (0, 0))],
        out_specs=pl.BlockSpec((chunks // 4, lead + extra, lanes), lambda i: (i, 0, 0)),
        out_shape=jax.ShapeDtypeStruct((chunks, lead + extra, lanes), F32),
        compiler_params=pltpu.CompilerParams(vmem_limit_bytes=16 * 2**20),
        name=name,
    )(mine, got, tail)


def spread_kernel(near_ref, mirror_ref, tile_ref, out_ref):
    for r in range(8):
        out_ref[r, :32, :] = near_ref[:32, :]
        out_ref[r, 32:64, :] = mirror_ref[...]
        out_ref[r, 64:72, :] = near_ref[32:40, :]
        out_ref[r, 72:, :] = tile_ref[16:, :]


def spread(near, mirror, tile):
    return pl.pallas_call(
        spread_kernel,
        out_shape=jax.ShapeDtypeStruct((8, 80, 128), F32),
        compiler_params=pltpu.CompilerParams(vmem_limit_bytes=16 * 2**20),
        name="spread",
    )(near, mirror, tile)


def blend_kernel(place_ref, rows_ref, fa_ref, fg_ref, na_ref, ng_ref, stat, *, total_rows):
    keep, fresh = decay_rate, 1.0 - decay_rate
    panel = place_ref[0]
    for c in range(16):
        cols = slice(64 * c, 64 * c + 64)
        k = (c - panel + 16) % 16

        @pl.when(k < 8)
        def _():
            block = rows_ref[k, :32, :]
            stat[:32, cols] = block[:, :64]
            stat[32:, cols] = block[:, 64:]

        @pl.when(k == 8)
        def _():
            half = 64 * (c % 2)
            stat[:, cols] = rows_ref[:, 64:72, :].reshape(64, 128)[:, half : half + 64]

        @pl.when(k > 8)
        def _():
            turned = rows_ref[16 - k, 32:64, :].T
            stat[:, 64 * c : 64 * c + 32] = turned[:64]
            stat[:, 64 * c + 32 : 64 * c + 64] = turned[64:]

    na_ref[...] = keep * fa_ref[...] + fresh * (stat[...] / total_rows)
    for y in range(4):
        r, c = slice(8 * (y // 2), 8 * (y // 2) + 8), slice(128 * (y % 2), 128 * (y % 2) + 128)
        ng_ref[r, c] = keep * fg_ref[r, c] + fresh * rows_ref[2 * y, 72:80, :]


def blend(place, rows, factor_a, factor_g, total_rows):
    return pl.pallas_call(
        lambda *refs: blend_kernel(*refs, total_rows=total_rows),
        in_specs=[in_smem()] + [in_vmem()] * 3,
        out_specs=[in_vmem()] * 2,
        out_shape=[jax.ShapeDtypeStruct(factor_a.shape, F32), jax.ShapeDtypeStruct(factor_g.shape, F32)],
        scratch_shapes=[pltpu.VMEM(factor_a.shape, F32)],
        compiler_params=pltpu.CompilerParams(vmem_limit_bytes=16 * 2**20),
        name="blend",
    )(place, rows, factor_a, factor_g)


def final_kernel(core_ref, inv_a_ref, own_ref, got_ref, inv_own_ref, inv_got_ref, out_ref, grad, inv_g):
    core = core_ref[0]
    for which, part, inv in ((core, own_ref, inv_own_ref), (1 - core, got_ref, inv_got_ref)):
        for q in range(8):
            owner = 2 * q + which
            rows = pl.ds(pl.multiple_of(owner * 64, 64), 64)
            for half in range(2):
                block = part[q * 8 : q * 8 + 8, half * 8 : half * 8 + 8, :]
                grad[rows, half * 128 : half * 128 + 128] = block.reshape(64, 128)
            for y in range(4):
                rows = pl.ds(pl.multiple_of(owner * 16 + 8 * (y // 2), 8), 8)
                inv_g[rows, 128 * (y % 2) : 128 * (y % 2) + 128] = inv[q * 8 + 2 * y]
    high = lax.Precision.HIGHEST
    left = jnp.dot(inv_a_ref[...], grad[...], precision=high, preferred_element_type=F32)
    out_ref[...] = jnp.dot(left, inv_g[...], precision=high, preferred_element_type=F32)


def final(core, inverse_a, own, got, inv_own, inv_got):
    cout = 256
    return pl.pallas_call(
        final_kernel,
        in_specs=[in_smem()] + [in_vmem()] * 5,
        out_specs=in_vmem(),
        out_shape=jax.ShapeDtypeStruct((inverse_a.shape[0], cout), F32),
        scratch_shapes=[pltpu.VMEM((inverse_a.shape[1], cout), F32), pltpu.VMEM((cout, cout), F32)],
        compiler_params=pltpu.CompilerParams(vmem_limit_bytes=16 * 2**20),
        name="final",
    )(core, inverse_a, own, got, inv_own, inv_got)


def twin(flat):
    return (flat // 16) * 16 + (flat + 8) % 16


def across(flat):
    panel, rep = flat // 8, flat % 8
    return (panel + rep) % 16 * 8 + rep


def swap(array, to=twin):
    return lax.ppermute(array, SUB, [(i, to(i)) for i in range(128)])


def exchange(array, axes):
    return lax.all_to_all(array, axes, 0, 0, tiled=True)


def local(activations, out_grads, factor_a, factor_g, inverse_a, inverse_g):
    total_rows = activations.shape[0] * 128
    core = lax.axis_index("co").astype(jnp.int32).reshape(1)
    place = lax.axis_index(("x", "zl", "co")).astype(jnp.int32).reshape(1)
    y = lax.axis_index("y")

    g_mine, g_other = grad_parts(core, activations, out_grads)
    tile = lax.dynamic_slice(inverse_g, (8 * (y // 2), 128 * (y % 2)), (8, 128))
    g_sum = pack(g_mine, swap(g_other), tile, 8, "grad_sum")
    g_sum, core = lax.optimization_barrier((g_sum, core))
    g_all = exchange(g_sum, CHIPS)

    s_mine, s_other = stat_parts(core, activations)
    g_all, s_mine, s_other = lax.optimization_barrier((g_all, s_mine, s_other))
    g_own = jnp.sum(g_all[:, :24], axis=0)
    inv_own = g_all[:, 24:]
    inv_got = swap(inv_own)
    s_sum = pack(s_mine, swap(s_other), g_own, 16, "stat_sum")
    s_sum, inv_got = lax.optimization_barrier((s_sum, inv_got))
    s_all = exchange(s_sum, CHIPS)

    near = jnp.sum(s_all[:, :40], axis=0)
    mirror = swap(near[:32], across)
    mirror, late = lax.optimization_barrier((mirror, s_all))
    own = late[:, 40:]
    got = swap(own)
    rows = exchange(spread(near, mirror, g_own), ("y", "zh"))
    precond_grad = final(core, inverse_a, own, got, inv_own, inv_got)
    rows, precond_grad = lax.optimization_barrier((rows, precond_grad))
    new_factor_a, new_factor_g = blend(place, rows, factor_a, factor_g, total_rows)
    return new_factor_a, new_factor_g, precond_grad


def solution(mesh):
    fine = jax.sharding.Mesh(mesh.devices.reshape(SIZES), SUB)
    rows = P(SUB, None)
    panel = P(("x", "zl", "co"), None)
    return jax.shard_map(
        local,
        mesh=fine,
        in_specs=(rows, rows, panel, panel, panel, panel),
        out_specs=(panel, panel, panel),
        check_vma=False,
    )
```
